512 devices in a mesh: chan: 64 (over z, y), rad: 8 (over x, core).
Axes of the slice: x: 4, y: 4, z: 16, core: 2. Of those that a mesh axis runs over, the one named last changes fastest.
Arguments:
- trial_block: float32 [1024, 16, 128], P('chan', None, 'rad')
- ham_blocks: bfloat16 [1024, 8, 128, 128], P('chan', None, 'rad'), may hold values from -0.1875 to 0.1875
- partners: int32 [1024, 8], P('chan'), may hold values from 0 to 1023, as said below
- stored_at: int32 [1024], replicated, may hold values from 0 to 1023, as said below
- precond_diag: float32 [1024, 128], P('chan', 'rad'), may hold values from 1 to 10
Outputs:
- new_block: float32 [1024, 16, 128], P('chan', None, 'rad')
- ritz_values: float32 [16], replicated
The draws below stay inside these ranges and needn't reach their ends.
Inputs may be any that keep to these rules, and one draw needn't show every extreme that they name: `stored_at`: A permutation of the channel numbers. `partners`: among the 128 entries of the rows p with p // 16 = d, for every d, at most 4 have stored_at[partner] // 16 equal to any one value; for every d some value has exactly 4.
All inputs are finite; a program needn't handle non-finite values.
Results may differ from the reference program's by a relative error of at most 0.0051.
Values may be sent and summed in bfloat16 or wider, within the bound.
A program may use at most 64 MiB of HBM per device.

```python
import math
import jax
import jax.numpy as jnp
from jax import lax

NCH = 1024
NB = 128
K = 16
NCOUP = 8
CH_DEV = 16
CAP = 4
N_CHAN = 64


def stored_perm(key):
    return jax.random.permutation(jax.random.fold_in(key, 11), NCH).astype(jnp.int32)


def draw_stored_at(key, part):
    return stored_perm(key)


def draw_partners(key, part):
    perm = stored_perm(key)
    inverse = jnp.argsort(perm, stable=True).astype(jnp.int32)
    requests = CH_DEV * NCOUP
    slots = N_CHAN * CAP
    slot_owner = jnp.arange(slots, dtype=jnp.int32) // CAP
    popular = jax.random.randint(jax.random.fold_in(key, 16), (N_CHAN,), 0, 4)
    priority = jax.random.randint(jax.random.fold_in(key, 12), (N_CHAN, slots), 0, 2 ** 27)
    priority = priority + (3 - popular[slot_owner])[None, :] * 2 ** 27
    forced = jax.random.randint(jax.random.fold_in(key, 13), (N_CHAN,), 0, N_CHAN)
    priority = jnp.where(slot_owner[None, :] == forced[:, None], -1, priority)
    chosen = jnp.argsort(priority, axis=1, stable=True)[:, :requests].astype(jnp.int32)
    shuffle_keys = jax.random.randint(jax.random.fold_in(key, 14), (N_CHAN, requests), 0, 2 ** 30)
    shuffle = jnp.argsort(shuffle_keys, axis=1, stable=True)
    chosen = jnp.take_along_axis(chosen, shuffle, axis=1)
    owner_dev = chosen // CAP
    local_row = jax.random.randint(jax.random.fold_in(key, 15), (N_CHAN, requests), 0, CH_DEV)
    channel = inverse[owner_dev * CH_DEV + local_row]
    return channel.reshape(NCH, NCOUP).astype(jnp.int32)


def draw_trial_block(key, part):
    position = jnp.arange(NCH, dtype=jnp.float32) / jnp.float32(NCH - 1)
    ramp = (3.0 ** (0.5 * position))[:, None, None]
    columns = jnp.exp(jax.random.uniform(jax.random.fold_in(key, 3), (1, K, 1), jnp.float32, 0.0, math.log(10.0)))
    rough = jnp.exp(jax.random.uniform(jax.random.fold_in(key, 2), (NCH, 1, NB), jnp.float32, 0.0, math.log(3.2)))
    base = jax.random.normal(jax.random.fold_in(key, 1), (NCH, K, NB), jnp.float32)
    return (base * ramp * rough * columns).astype(jnp.float32)


def levels(rng, shape, split, smallest, high):
    def one(axis_at, blocks):
        steps = jax.random.uniform(jax.random.fold_in(jax.random.fold_in(rng, 6), axis_at), (blocks,), jnp.float32, smallest / len(split), high / len(split))
        return jnp.repeat(jnp.exp(steps), shape[axis_at] // blocks).reshape((-1,) + (1,) * (len(shape) - axis_at - 1))

    loudness = one(*split[0])
    for cut in split[1:]:
        loudness = loudness * one(*cut)
    return loudness


def scatter_about(rng, shape, spread, limit, split=(), kind=jnp.bfloat16):
    values = spread * jax.random.normal(rng, shape, jnp.float32)
    if split:
        values = values * levels(rng, shape, split, -0.22, 0.18)
    return jnp.clip(values, -limit, limit).astype(kind)


def setup_inputs(seed: int = 0) -> dict:
    key_list = jax.random.split(jax.random.key(seed), 6)
    return {
        "trial_block": draw_trial_block(jax.random.fold_in(key_list[5], 71), 0),
        "ham_blocks": scatter_about(key_list[1], (NCH, NCOUP, NB, NB), (NCOUP * NB) ** -0.5, 0.1875, ((0, 64), (2, 8))),
        "partners": draw_partners(jax.random.fold_in(key_list[5], 71), 0),
        "stored_at": draw_stored_at(jax.random.fold_in(key_list[5], 71), 0),
        "precond_diag": jnp.clip(jnp.exp(math.log(10.0) - 2.3025851 * jax.random.uniform(key_list[4], (NCH, NB), jnp.float32) ** levels(key_list[4], (NCH, NB), ((0, 64), (1, 8)), -0.2, 0.2)), 1.0, 10.0),
    }


def chol_solve(factor, rhs):
    first = lax.linalg.triangular_solve(factor, rhs, left_side=True, lower=True)
    return lax.linalg.triangular_solve(factor, first, left_side=True, lower=True, transpose_a=True)

def inner_products(left, right):
    return jnp.einsum('pkr,plr->kl', left, right, precision=lax.Precision.HIGHEST)

def reference(trial_block, ham_blocks, partners, stored_at, precond_diag):
    rounded = trial_block.astype(jnp.bfloat16)
    rows_used = stored_at[partners].astype(jnp.int32)
    coupled = rounded[rows_used]
    applied = jnp.einsum('cjks,cjrs->ckr', coupled.astype(jnp.float32), ham_blocks.astype(jnp.float32), precision=lax.Precision.HIGHEST)
    proj_a = inner_products(trial_block, applied)
    proj_b = inner_products(trial_block, trial_block)
    factor = jnp.linalg.cholesky(proj_b)
    coefficients = chol_solve(factor, proj_a)
    ritz_values = jnp.diagonal(coefficients)
    residual = applied - jnp.einsum('pkr,kl->plr', trial_block, coefficients, precision=lax.Precision.HIGHEST)
    correction = residual / precond_diag[:, None, :]
    correlation = inner_products(trial_block, correction)
    mixing = chol_solve(factor, correlation)
    projected = correction - jnp.einsum('pkr,kl->plr', trial_block, mixing, precision=lax.Precision.HIGHEST)
    correlation_gram = inner_products(projected, projected) / jnp.float32(NCH * NB)
    gram_factor = jnp.linalg.cholesky(correlation_gram)
    flat_rows = jnp.transpose(projected, (1, 0, 2)).reshape(K, -1)
    solved = lax.linalg.triangular_solve(gram_factor, flat_rows, left_side=True, lower=True)
    new_block = jnp.transpose(solved.reshape(K, NCH, NB), (1, 0, 2))
    return (new_block, ritz_values)
```

```python
import jax
import jax.numpy as jnp
from jax import lax
from jax.experimental import pallas as pl
from jax.experimental.pallas import tpu as pltpu
from jax.sharding import PartitionSpec as P

MESH = pl.DeviceIdType.MESH
HI = lax.Precision.HIGHEST
F32 = jnp.float32
BF16 = jnp.bfloat16
TOTAL_ROWS = 1024.0 * 128.0
NJ = 8
CHUNK = 4


def kernel(t_ref, ham_ref, partners_ref, stored_ref, d_ref, new_ref, ritz_ref,
           hbuf, tbl, yall, red1, red2, red3,
           ham_sem, far_s, far_r, mid_s, mid_r, last_s, last_r, x_s, x_r, c_s, c_r, r1_s, r1_r, r2_s, r2_r, r3_s, r3_r):
    chan = lax.axis_index("chan")
    rad = lax.axis_index("rad")
    z, y = chan // 4, chan % 4
    zc, zf = z % 4, z // 4
    two = 2 - 4 * (z % 2)

    ham_copy = pltpu.make_async_copy(ham_ref, hbuf, ham_sem)
    ham_copy.start()

    def at(dz, yy):
        return (((z + dz + 16) % 16) * 4 + yy, rad)

    near = (0, 1, -1, two)
    barrier = pltpu.get_barrier_semaphore()
    met = 0
    for i in range(1, 8):
        pl.semaphore_signal(barrier, inc=1, device_id=(chan, rad ^ i), device_id_type=MESH)
        met += 1
    for m in range(1, 4):
        pl.semaphore_signal(barrier, inc=1, device_id=at(4 * m, y), device_id_type=MESH)
        met += 1
    for dy in range(4):
        for dz in (-2, -1, 0, 1, 2):
            if dy or dz:
                pl.semaphore_signal(barrier, inc=1, device_id=at(dz, y ^ dy), device_id_type=MESH)
                met += 1

    slot0 = y * 16 + zc * 4 + zf
    slot1 = zc * 16 + y * 4 + zf
    t2d = t_ref[...].reshape(256, 16)
    eye = (lax.broadcasted_iota(jnp.int32, (16, 16), 0) == lax.broadcasted_iota(jnp.int32, (16, 16), 1)).astype(BF16)
    turned = lax.dot_general(eye, t2d.astype(BF16), (((1,), (1,)), ((), ())), preferred_element_type=F32).astype(BF16)
    tbl[slot0] = turned[:, :128]
    tbl[64 + slot1] = turned[:, 128:]

    pl.semaphore_wait(barrier, met)

    def remote(src, dst, s, r, dev):
        copy = pltpu.make_async_remote_copy(src_ref=src, dst_ref=dst, send_sem=s, recv_sem=r,
                                            device_id=dev, device_id_type=MESH)
        copy.start()
        return copy

    far = []
    for m in range(1, 4):
        for h, slot in ((0, slot0), (1, 64 + slot1)):
            i = (m - 1) * 2 + h
            piece = tbl.at[pl.ds(slot, 1)]
            far.append(remote(piece, piece, far_s.at[i], far_r.at[i], at(4 * m, y)))

    t2 = jnp.concatenate([t_ref[p] for p in range(16)], axis=1)
    d2 = jnp.concatenate([d_ref[p:p + 1, :] for p in range(16)], axis=1)
    td = t2 / d2

    for c in far:
        c.wait_recv()
    mid = []
    for n in range(1, 4):
        piece = tbl.at[pl.ds(y * 16 + zc * 4, 4)]
        mid.append(remote(piece, piece, mid_s.at[n - 1], mid_r.at[n - 1], at(near[n], y)))
        piece = tbl.at[pl.ds(64 + zc * 16 + y * 4, 4)]
        mid.append(remote(piece, piece, mid_s.at[n + 2], mid_r.at[n + 2], at(0, y ^ n)))
    for c in mid:
        c.wait_recv()
    last = []
    for n in range(1, 4):
        piece = tbl.at[pl.ds(y * 16, 16)]
        last.append(remote(piece, piece, last_s.at[n - 1], last_r.at[n - 1], at(0, y ^ n)))
        piece = tbl.at[pl.ds(64 + zc * 16, 16)]
        last.append(remote(piece, piece, last_s.at[n + 2], last_r.at[n + 2], at(near[n], y)))
    for c in last:
        c.wait_recv()

    lane_group = lax.broadcasted_iota(jnp.int32, (16, 128), 1) // 16

    def select(j, carry):
        for hp in range(2):
            acc = jnp.zeros((16, 128), F32)
            for g in range(8):
                row = stored_ref[partners_ref[hp * 8 + g, j]]
                dev = row // 16
                rz, ry = dev // 4, dev % 4
                first = ry * 16 + (rz % 4) * 4 + rz // 4
                second = 64 + (rz % 4) * 16 + ry * 4 + rz // 4
                half = (row // 8) % 2
                tile = tbl[first + half * (second - first)].astype(F32)
                moved = pltpu.roll(tile, ((g - row % 8 + 8) % 8) * 16, 1)
                acc = jnp.where(lane_group == g, moved, acc)
            yall[j, rad, :, hp * 128:(hp + 1) * 128] = acc.astype(BF16)
        return carry

    other = (chan, rad ^ 1)
    along_x, across = [], []
    for c in range(NJ // CHUNK):
        lax.fori_loop(c * CHUNK, (c + 1) * CHUNK, select, 0)
        piece = yall.at[pl.ds(c * CHUNK, CHUNK), pl.ds(rad, 1)]
        for i in range(1, 4):
            k = c * 3 + i - 1
            along_x.append(remote(piece, piece, x_s.at[k], x_r.at[k], (chan, rad ^ (2 * i))))
        across.append(remote(piece, piece, c_s.at[c * 4], c_r.at[c * 4], other))

    ham_copy.wait()
    out_group = lax.broadcasted_iota(jnp.int32, (16, 256), 1) // 16
    applied_r = jnp.zeros((16, 256), F32)
    for c in range(NJ // CHUNK):
        for i in range(1, 4):
            along_x[c * 3 + i - 1].wait_recv()
            piece = yall.at[pl.ds(c * CHUNK, CHUNK), pl.ds(rad ^ (2 * i), 1)]
            across.append(remote(piece, piece, c_s.at[c * 4 + i], c_r.at[c * 4 + i], other))
    n_chunks = NJ // CHUNK
    for c in range(n_chunks):
        across[c].wait_recv()
        for i in range(3):
            across[n_chunks + c * 3 + i].wait_recv()
        js = range(c * CHUNK, (c + 1) * CHUNK)
        left = jnp.concatenate([hbuf[:, j].reshape(256, 128) for j in js], axis=1)
        right = yall[c * CHUNK:(c + 1) * CHUNK].reshape(CHUNK * 128, 256)
        out = jnp.dot(left, right, preferred_element_type=F32)
        for p in range(16):
            applied_r += jnp.where(out_group == p, out[p * 16:(p + 1) * 16, :], 0.0)

    turned_a = applied_r.T
    a2 = jnp.concatenate([turned_a[p * 16:(p + 1) * 16, :] for p in range(16)], axis=1)
    ad = a2 / d2

    left = jnp.concatenate([t2, td, ad], axis=0)
    right = jnp.concatenate([t2, a2, td, ad], axis=0)
    prods = lax.dot_general(left, right, (((1,), (1,)), ((), ())), precision=HI, preferred_element_type=F32)
    prods = jnp.concatenate([prods, jnp.zeros((48, 64), F32)], axis=1)
    lane = lax.broadcasted_iota(jnp.int32, (16, 128), 1)
    top = jnp.where(lane < 64, prods[:16], 0.0)
    second = jnp.where((lane >= 64) & (lane < 96), pltpu.roll(prods[16:32], 32, 1), 0.0)
    third = jnp.where((lane >= 96) & (lane < 112), pltpu.roll(prods[32:48], 48, 1), 0.0)
    mine = top + second + third

    red1[rad] = mine
    sums = []
    for i in range(1, 8):
        piece = red1.at[pl.ds(rad, 1)]
        sums.append(remote(piece, piece, r1_s.at[i - 1], r1_r.at[i - 1], (chan, rad ^ i)))
    for c in sums:
        c.wait_recv()
    total = red1[0]
    for i in range(1, 8):
        total = total + red1[i]

    red2[zf] = total
    for m in range(1, 4):
        piece = red2.at[pl.ds(zf, 1)]
        sums.append(remote(piece, piece, r2_s.at[m - 1], r2_r.at[m - 1], at(4 * m, y)))
    for c in sums[7:]:
        c.wait_recv()
    total = (red2[0] + red2[1]) + (red2[2] + red2[3])

    red3[y * 4 + zc] = total
    for dy in range(4):
        for n in range(4):
            if dy or n:
                i = dy * 4 + n - 1
                piece = red3.at[pl.ds(y * 4 + zc, 1)]
                sums.append(remote(piece, piece, r3_s.at[i], r3_r.at[i], at(near[n], y ^ dy)))
    for c in sums[10:]:
        c.wait_recv()
    total = red3[0]
    for i in range(1, 16):
        total = total + red3[i]

    rows = lax.broadcasted_iota(jnp.int32, (16, 128), 0)

    def block(m, b):
        return (pltpu.roll(m, 128 - 16 * b, 1) if b else m)[:, :16]

    m = total
    for i in range(16):
        pivot_row = m[i:i + 1, :] / m[i:i + 1, i:i + 1]
        m = jnp.where(rows == i, pivot_row, m - m[:, i:i + 1] * pivot_row)
    coef = block(m, 1)
    q_ta = block(total, 5)
    level = jnp.dot(jnp.concatenate([block(total, 2), block(m, 2), block(total, 4)], axis=0), coef,
                    precision=HI, preferred_element_type=F32)
    corr = block(total, 3) - level[:16]
    mixing = block(m, 3) - level[16:32]
    inner = level[32:48] - q_ta
    tn = (((0,), (0,)), ((), ()))
    gram = block(total, 6) + lax.dot_general(jnp.concatenate([-q_ta, coef, -corr], axis=0),
                                             jnp.concatenate([coef, inner, mixing], axis=0), tn,
                                             precision=HI, preferred_element_type=F32)
    gram = gram / TOTAL_ROWS
    projected = ad - lax.dot_general(jnp.concatenate([coef, mixing], axis=0), jnp.concatenate([td, t2], axis=0), tn,
                                     precision=HI, preferred_element_type=F32)
    small = (16, 16)
    diagonal = lax.broadcasted_iota(jnp.int32, small, 0) == lax.broadcasted_iota(jnp.int32, small, 1)
    ritz_ref[...] = jnp.sum(jnp.where(diagonal, coef, 0.0), axis=0, keepdims=True)

    e = jnp.concatenate([gram, jnp.where(diagonal, 1.0, 0.0), jnp.zeros((16, 96), F32)], axis=1)
    for i in range(15):
        e = e - jnp.where(rows > i, e[:, i:i + 1] / e[i:i + 1, i:i + 1], 0.0) * e[i:i + 1, :]
    pivots = jnp.sum(jnp.where(rows == lane, e, 0.0), axis=1, keepdims=True)
    inv_factor = block(e * lax.rsqrt(pivots), 1)
    new = jnp.dot(inv_factor, projected, precision=HI, preferred_element_type=F32)
    for p in range(16):
        half = new[:, (p // 8) * 128:(p // 8 + 1) * 128]
        g = p % 8
        new_ref[p] = (pltpu.roll(half, 128 - 16 * g, 1) if g else half)[:, :16]

    for c in far + mid + last + along_x + across + sums:
        c.wait_send()


def body(trial_block, ham_blocks, partners, stored_at, precond_diag):
    vmem = pl.BlockSpec(memory_space=pltpu.VMEM)
    smem = pl.BlockSpec(memory_space=pltpu.SMEM)
    dma = pltpu.SemaphoreType.DMA
    n_chunks = NJ // CHUNK
    counts = (6, 6, 6, 6, 6, 6, 3 * n_chunks, 3 * n_chunks, 4 * n_chunks, 4 * n_chunks, 7, 7, 3, 3, 15, 15)
    new_block, ritz = pl.pallas_call(
        kernel,
        out_shape=(jax.ShapeDtypeStruct((16, 16, 16), F32), jax.ShapeDtypeStruct((1, 16), F32)),
        in_specs=[vmem, pl.BlockSpec(memory_space=pl.ANY), smem, smem, vmem],
        out_specs=(vmem, vmem),
        scratch_shapes=[
            pltpu.VMEM((16, 8, 16, 128), BF16),
            pltpu.VMEM((128, 16, 128), BF16),
            pltpu.VMEM((8, 8, 16, 256), BF16),
            pltpu.VMEM((8, 16, 128), F32),
            pltpu.VMEM((4, 16, 128), F32),
            pltpu.VMEM((16, 16, 128), F32),
            dma,
            *[dma((n,)) for n in counts],
        ],
        compiler_params=pltpu.CompilerParams(collective_id=0, has_side_effects=True, vmem_limit_bytes=32 * 2**20),
    )(trial_block, ham_blocks, partners, stored_at, precond_diag)
    return new_block, ritz.reshape(16)


def solution(mesh):
    return jax.shard_map(
        body,
        mesh=mesh,
        in_specs=(
            P("chan", None, "rad"),
            P("chan", None, "rad", None),
            P("chan", None),
            P(),
            P("chan", "rad"),
        ),
        out_specs=(P("chan", None, "rad"), P()),
        check_vma=False,
    )
```

```python
import jax
import jax.numpy as jnp
from jax import lax
from jax.experimental import pallas as pl
from jax.experimental.pallas import tpu as pltpu
from jax.sharding import PartitionSpec as P

MESH = pl.DeviceIdType.MESH
HI = lax.Precision.HIGHEST
F32 = jnp.float32
BF16 = jnp.bfloat16
TOTAL_ROWS = 1024.0 * 128.0
NJ = 8
CHUNK = 2


def kernel(t_hbm, ham_hbm, partners_hbm, stored_hbm, d_hbm, new_ref, ritz_ref,
           t_ref, d_ref, hbuf, partners_ref, stored_ref, place, tbl, yall, red1, red2, red3,
           in_sem, far_s, far_r, own_s, own_r, fwd_s, fwd_r, x_s, x_r, c_s, c_r, r1_s, r1_r, r2_s, r2_r, r3_s, r3_r):
    chan = lax.axis_index("chan")
    rad = lax.axis_index("rad")
    z, y = chan // 4, chan % 4
    zc, zf = z % 4, z // 4
    two = 2 - 4 * (z % 2)

    def at(dz, yy):
        return (((z + dz + 16) % 16) * 4 + yy, rad)

    t_copy = pltpu.make_async_copy(t_hbm, t_ref, in_sem.at[0])
    t_copy.start()
    near = (0, 1, -1, two)
    barrier = pltpu.get_barrier_semaphore()
    met = 0
    for m in (2, 1, 3):
        pl.semaphore_signal(barrier, inc=1, device_id=at(4 * m, y), device_id_type=MESH)
        met += 1
    for dy in range(4):
        for dz in (-2, -1, 0, 1, 2):
            if dy or dz:
                pl.semaphore_signal(barrier, inc=1, device_id=at(dz, y ^ dy), device_id_type=MESH)
                met += 1
    for i in range(1, 8):
        pl.semaphore_signal(barrier, inc=1, device_id=(chan, rad ^ i), device_id_type=MESH)
        met += 1
    rest = [pltpu.make_async_copy(src, dst, in_sem.at[i + 1]) for i, (src, dst) in enumerate(
        ((d_hbm, d_ref), (partners_hbm, partners_ref), (stored_hbm, stored_ref), (ham_hbm, hbuf)))]
    for c in rest:
        c.start()

    slot0 = y * 16 + zc * 4 + zf
    slot1 = 64 + zc * 16 + y * 4 + zf
    t_copy.wait()
    t2d = t_ref[...].reshape(256, 16)
    eye = (lax.broadcasted_iota(jnp.int32, (16, 16), 0) == lax.broadcasted_iota(jnp.int32, (16, 16), 1)).astype(BF16)
    turned = lax.dot_general(eye, t2d.astype(BF16), (((1,), (1,)), ((), ())), preferred_element_type=F32).astype(BF16)
    tbl[slot0] = turned[:, :128]
    tbl[slot1] = turned[:, 128:]

    pl.semaphore_wait(barrier, met)

    def remote(src, dst, s, r, dev):
        copy = pltpu.make_async_remote_copy(src_ref=src, dst_ref=dst, send_sem=s, recv_sem=r,
                                            device_id=dev, device_id_type=MESH)
        copy.start()
        return copy

    far = []
    for m in (2, 1, 3):
        for h, slot in ((0, slot0), (1, slot1)):
            i = (m - 1) * 2 + h
            piece = tbl.at[pl.ds(slot, 1)]
            far.append(remote(piece, piece, far_s.at[i], far_r.at[i], at(4 * m, y)))

    for c in rest:
        c.wait()
    t2 = jnp.concatenate([t_ref[p] for p in range(16)], axis=1)
    d2 = jnp.concatenate([d_ref[p:p + 1, :] for p in range(16)], axis=1)
    td = t2 / d2

    def locate(j, carry):
        for p in range(16):
            row = stored_ref[partners_ref[j, p]]
            ry, rc, rf = (row // 16) % 4, (row // 64) % 4, row // 256
            half = (row // 8) % 2
            place[j * 16 + p] = half * (64 + rc * 16 + ry * 4) + (1 - half) * (ry * 16 + rc * 4) + rf
            place[128 + j * 16 + p] = ((p - row + 16) % 8) * 16
        return carry

    lax.fori_loop(0, NJ, locate, 0)

    for c in far:
        c.wait_recv()
    sent = []

    def hand_on(h, first, group, k, sems):
        piece = tbl.at[pl.ds(first, 4)]
        to = at(near[k], y) if group == "z" else at(0, y ^ k)
        s, r, i = sems
        copy = remote(piece, piece, s.at[i], r.at[i], to)
        sent.append(copy)
        return copy

    own0, own1 = y * 16 + zc * 4, 64 + zc * 16 + y * 4
    first_z, first_y, second_z, second_y = {}, {}, {}, {}
    for k in (3, 1, 2):
        first_z[k] = hand_on(0, own0, "z", k, (own_s, own_r, k - 1))
    for k in (2, 1, 3):
        second_y[k] = hand_on(1, own1, "y", k, (own_s, own_r, 3 + k - 1))
    for k in (2, 1, 3):
        first_y[k] = hand_on(0, own0, "y", k, (own_s, own_r, 6 + k - 1))
    for k in (3, 1, 2):
        second_z[k] = hand_on(1, own1, "z", k, (own_s, own_r, 9 + k - 1))
    onward = []
    for n, d in ((1, 1), (2, 3), (3, 2)):
        first_z[n].wait_recv()
        came = y * 16 + ((z - near[n] + 16) % 4) * 4
        for k in (2, 1, 3):
            onward.append(hand_on(0, came, "y", k, (fwd_s, fwd_r, (n - 1) * 3 + k - 1)))
        second_y[d].wait_recv()
        came = 64 + zc * 16 + (y ^ d) * 4
        for k in (3, 1, 2):
            onward.append(hand_on(1, came, "z", k, (fwd_s, fwd_r, 9 + (d - 1) * 3 + k - 1)))
    for c in [*first_y.values(), *second_z.values(), *onward]:
        c.wait_recv()

    lane_group = lax.broadcasted_iota(jnp.int32, (16, 128), 1) // 16

    def select(j, carry):
        for hp in range(2):
            acc = jnp.zeros((16, 128), F32)
            for g in range(8):
                i = j * 16 + hp * 8 + g
                moved = pltpu.roll(tbl[place[i]].astype(F32), place[128 + i], 1)
                acc = jnp.where(lane_group == g, moved, acc)
            yall[j, rad, :, hp * 128:(hp + 1) * 128] = acc.astype(BF16)
        return carry

    other = (chan, rad ^ 1)
    along_x, across = {}, {}
    n_chunks = NJ // CHUNK
    for c in range(n_chunks):
        lax.fori_loop(c * CHUNK, (c + 1) * CHUNK, select, 0)
        piece = yall.at[pl.ds(c * CHUNK, CHUNK), pl.ds(rad, 1)]
        for i in (2, 1, 3):
            k = c * 3 + i - 1
            along_x[c, i] = remote(piece, piece, x_s.at[k], x_r.at[k], (chan, rad ^ (2 * i)))
        across[c, 0] = remote(piece, piece, c_s.at[c * 4], c_r.at[c * 4], other)

    out_group = lax.broadcasted_iota(jnp.int32, (16, 256), 1) // 16
    applied_r = jnp.zeros((16, 256), F32)
    for c in range(n_chunks + 1):
        if c < n_chunks:
            for i in (1, 3, 2):
                along_x[c, i].wait_recv()
                piece = yall.at[pl.ds(c * CHUNK, CHUNK), pl.ds(rad ^ (2 * i), 1)]
                across[c, i] = remote(piece, piece, c_s.at[c * 4 + i], c_r.at[c * 4 + i], other)
        if c:
            for i in range(4):
                across[c - 1, i].wait_recv()
            js = range((c - 1) * CHUNK, c * CHUNK)
            left = jnp.concatenate([hbuf[:, j].reshape(256, 128) for j in js], axis=1)
            right = yall[(c - 1) * CHUNK:c * CHUNK].reshape(CHUNK * 128, 256)
            out = jnp.dot(left, right, preferred_element_type=F32)
            for p in range(16):
                applied_r += jnp.where(out_group == p, out[p * 16:(p + 1) * 16, :], 0.0)

    turned_a = applied_r.T
    a2 = jnp.concatenate([turned_a[p * 16:(p + 1) * 16, :] for p in range(16)], axis=1)
    ad = a2 / d2

    left = jnp.concatenate([t2, td, ad], axis=0)
    right = jnp.concatenate([t2, a2, td, ad], axis=0)
    prods = lax.dot_general(left, right, (((1,), (1,)), ((), ())), precision=HI, preferred_element_type=F32)
    prods = jnp.concatenate([prods, jnp.zeros((48, 64), F32)], axis=1)
    lane = lax.broadcasted_iota(jnp.int32, (16, 128), 1)
    top = jnp.where(lane < 64, prods[:16], 0.0)
    second = jnp.where((lane >= 64) & (lane < 96), pltpu.roll(prods[16:32], 32, 1), 0.0)
    third = jnp.where((lane >= 96) & (lane < 112), pltpu.roll(prods[32:48], 48, 1), 0.0)
    mine = top + second + third

    red1[rad] = mine
    sums = []
    for i in range(1, 8):
        piece = red1.at[pl.ds(rad, 1)]
        sums.append(remote(piece, piece, r1_s.at[i - 1], r1_r.at[i - 1], (chan, rad ^ i)))
    for c in sums:
        c.wait_recv()
    total = red1[0]
    for i in range(1, 8):
        total = total + red1[i]

    red2[zf] = total
    for m in range(1, 4):
        piece = red2.at[pl.ds(zf, 1)]
        sums.append(remote(piece, piece, r2_s.at[m - 1], r2_r.at[m - 1], at(4 * m, y)))
    for c in sums[7:]:
        c.wait_recv()
    total = (red2[0] + red2[1]) + (red2[2] + red2[3])

    red3[y * 4 + zc] = total
    for dy in range(4):
        for n in range(4):
            if dy or n:
                i = dy * 4 + n - 1
                piece = red3.at[pl.ds(y * 4 + zc, 1)]
                sums.append(remote(piece, piece, r3_s.at[i], r3_r.at[i], at(near[n], y ^ dy)))
    for c in sums[10:]:
        c.wait_recv()
    total = red3[0]
    for i in range(1, 16):
        total = total + red3[i]

    rows = lax.broadcasted_iota(jnp.int32, (16, 128), 0)

    def block(m, b):
        return (pltpu.roll(m, 128 - 16 * b, 1) if b else m)[:, :16]

    m = total
    for i in range(16):
        pivot_row = m[i:i + 1, :] / m[i:i + 1, i:i + 1]
        m = jnp.where(rows == i, pivot_row, m - m[:, i:i + 1] * pivot_row)
    coef = block(m, 1)
    q_ta = block(total, 5)
    level = jnp.dot(jnp.concatenate([block(total, 2), block(m, 2), block(total, 4)], axis=0), coef,
                    precision=HI, preferred_element_type=F32)
    corr = block(total, 3) - level[:16]
    mixing = block(m, 3) - level[16:32]
    inner = level[32:48] - q_ta
    tn = (((0,), (0,)), ((), ()))
    gram = block(total, 6) + lax.dot_general(jnp.concatenate([-q_ta, coef, -corr], axis=0),
                                             jnp.concatenate([coef, inner, mixing], axis=0), tn,
                                             precision=HI, preferred_element_type=F32)
    gram = gram / TOTAL_ROWS
    projected = ad - lax.dot_general(jnp.concatenate([coef, mixing], axis=0), jnp.concatenate([td, t2], axis=0), tn,
                                     precision=HI, preferred_element_type=F32)
    small = (16, 16)
    diagonal = lax.broadcasted_iota(jnp.int32, small, 0) == lax.broadcasted_iota(jnp.int32, small, 1)
    ritz_ref[...] = jnp.sum(jnp.where(diagonal, coef, 0.0), axis=0, keepdims=True)

    e = jnp.concatenate([gram, jnp.where(diagonal, 1.0, 0.0), jnp.zeros((16, 96), F32)], axis=1)
    for i in range(15):
        e = e - jnp.where(rows > i, e[:, i:i + 1] / e[i:i + 1, i:i + 1], 0.0) * e[i:i + 1, :]
    pivots = jnp.sum(jnp.where(rows == lane, e, 0.0), axis=1, keepdims=True)
    inv_factor = block(e * lax.rsqrt(pivots), 1)
    new = jnp.dot(inv_factor, projected, precision=HI, preferred_element_type=F32)
    for p in range(16):
        half = new[:, (p // 8) * 128:(p // 8 + 1) * 128]
        g = p % 8
        new_ref[p] = (pltpu.roll(half, 128 - 16 * g, 1) if g else half)[:, :16]

    for c in [*far, *sent, *along_x.values(), *across.values(), *sums]:
        c.wait_send()


def body(trial_block, ham_blocks, partners, stored_at, precond_diag):
    vmem = pl.BlockSpec(memory_space=pltpu.VMEM)
    hbm = pl.BlockSpec(memory_space=pltpu.HBM)
    dma = pltpu.SemaphoreType.DMA
    n_chunks = NJ // CHUNK
    counts = (5, 6, 6, 12, 12, 18, 18, 3 * n_chunks, 3 * n_chunks, 4 * n_chunks, 4 * n_chunks, 7, 7, 3, 3, 15, 15)
    new_block, ritz = pl.pallas_call(
        kernel,
        out_shape=(jax.ShapeDtypeStruct((16, 16, 16), F32), jax.ShapeDtypeStruct((1, 16), F32)),
        in_specs=[hbm] * 5,
        out_specs=(vmem, vmem),
        scratch_shapes=[
            pltpu.VMEM((16, 16, 16), F32),
            pltpu.VMEM((16, 16), F32),
            pltpu.VMEM((16, 8, 16, 128), BF16),
            pltpu.SMEM((8, 16), jnp.int32),
            pltpu.SMEM((1024,), jnp.int32),
            pltpu.SMEM((256,), jnp.int32),
            pltpu.VMEM((128, 16, 128), BF16),
            pltpu.VMEM((8, 8, 16, 256), BF16),
            pltpu.VMEM((8, 16, 128), F32),
            pltpu.VMEM((4, 16, 128), F32),
            pltpu.VMEM((16, 16, 128), F32),
            *[dma((n,)) for n in counts],
        ],
        compiler_params=pltpu.CompilerParams(collective_id=0, has_side_effects=True, vmem_limit_bytes=60 * 2**20),
    )(trial_block, ham_blocks, partners.T, stored_at, precond_diag)
    return new_block, ritz.reshape(16)


def solution(mesh):
    return jax.shard_map(
        body,
        mesh=mesh,
        in_specs=(
            P("chan", None, "rad"),
            P("chan", None, "rad", None),
            P("chan", None),
            P(),
            P("chan", "rad"),
        ),
        out_specs=(P("chan", None, "rad"), P()),
        check_vma=False,
    )
```

```python
import functools

import jax
import jax.numpy as jnp
from jax import lax
from jax.experimental import pallas as pl
from jax.experimental.pallas import tpu as pltpu
from jax.sharding import PartitionSpec as P

MESH = pl.DeviceIdType.MESH
HI = lax.Precision.HIGHEST
F32 = jnp.float32
BF16 = jnp.bfloat16
TOTAL_ROWS = 1024.0 * 128.0
NJ = 8
ALONG_Z = (8, 7, 9, 6, 10, 5, 11, 4, 12, 3, 13, 2, 14, 1, 15)
IN_PLANE = sorted(((dy, dr) for dy in range(4) for dr in range(8) if dy or dr),
                  key=lambda d: -((0, 1, 2, 1)[d[0]] + (0, 1, 2, 1)[d[1] // 2]))
GROUPS = ((0, 4), (4, 8), (8, 12), (12, 16))
CHUNK = 4


def by_distance(d):
    return 2 * d - 1 if 0 < d <= 8 else 2 * (16 - d) % 32


def kernel(t_hbm, ham_hbm, partners_hbm, stored_hbm, d_hbm, new_ref, ritz_ref,
           t_ref, d_ref, hbuf, partners_ref, stored_ref, place, tbl, yall, trial1, trial2, red1, red2,
           in_sem, far_s, far_r, own_s, own_r, x_s, x_r, c_s, c_r,
           t1_s, t1_r, t2_s, t2_r, r1_s, r1_r, r2_s, r2_r):
    chan = lax.axis_index("chan")
    rad = lax.axis_index("rad")
    z, y = chan // 4, chan % 4

    def at(dz, yy):
        return (((z + dz + 16) % 16) * 4 + yy, rad)

    t_copy = pltpu.make_async_copy(t_hbm, t_ref, in_sem.at[0])
    t_copy.start()
    barrier = pltpu.get_barrier_semaphore()
    for m in ALONG_Z:
        pl.semaphore_signal(barrier, inc=1, device_id=at(m, y), device_id_type=MESH)
    for dy, dr in IN_PLANE:
        pl.semaphore_signal(barrier, inc=1, device_id=(z * 4 + (y ^ dy), rad ^ dr), device_id_type=MESH)
    rest = [pltpu.make_async_copy(src, dst, in_sem.at[i + 1]) for i, (src, dst) in enumerate(
        ((d_hbm, d_ref), (partners_hbm, partners_ref), (stored_hbm, stored_ref), (ham_hbm, hbuf)))]
    for c in rest:
        c.start()

    t_copy.wait()
    t2d = t_ref[...].reshape(256, 16)
    eye = (lax.broadcasted_iota(jnp.int32, (16, 16), 0) == lax.broadcasted_iota(jnp.int32, (16, 16), 1)).astype(BF16)
    turned = lax.dot_general(eye, t2d.astype(BF16), (((1,), (1,)), ((), ())), preferred_element_type=F32).astype(BF16)
    tbl[y * 16, 0] = turned[:, :128]
    tbl[y * 16, 1] = turned[:, 128:]

    pl.semaphore_wait(barrier, len(ALONG_Z) + len(IN_PLANE))

    def remote(src, dst, s, r, dev):
        copy = pltpu.make_async_remote_copy(src_ref=src, dst_ref=dst, send_sem=s, recv_sem=r,
                                            device_id=dev, device_id_type=MESH)
        copy.start()
        return copy

    far = {}
    for m in ALONG_Z:
        far[by_distance(16 - m)] = remote(tbl.at[pl.ds(y * 16, 1)], tbl.at[pl.ds(y * 16 + by_distance(16 - m), 1)],
                                          far_s.at[m], far_r.at[m], at(m, y))

    for c in rest:
        c.wait()
    t2 = jnp.concatenate([t_ref[p] for p in range(16)], axis=1)
    d2 = jnp.concatenate([d_ref[p:p + 1, :] for p in range(16)], axis=1)
    td = t2 / d2

    def pack(m):
        left_half = lax.broadcasted_iota(jnp.int32, (8, 128), 1) < 64
        return jnp.where(left_half, m[:8], pltpu.roll(m[8:], 64, 1))

    def unpack(m):
        return jnp.concatenate([m, pltpu.roll(m, 64, 1)], axis=0)

    def widen(m):
        return jnp.concatenate([m, jnp.zeros((m.shape[0], 128 - m.shape[1]), F32)], axis=1)

    sums = []

    def to_plane(buf, s, r):
        piece = buf.at[pl.ds(y * 8 + rad, 1)]
        return [remote(piece, piece, s.at[i], r.at[i], (z * 4 + (y ^ dy), rad ^ dr))
                for i, (dy, dr) in enumerate(IN_PLANE)]

    def to_planes(buf, s, r):
        piece = buf.at[pl.ds(z, 1)]
        return [remote(piece, piece, s.at[m], r.at[m], at(m, y)) for m in ALONG_Z]

    def summed(buf, copies):
        for c in copies:
            c.wait_recv()
        sums.extend(copies)
        parts = [buf[i] for i in range(buf.shape[0])]
        while len(parts) > 1:
            parts = [u + v for u, v in zip(parts[::2], parts[1::2])]
        return parts[0]

    lane = lax.broadcasted_iota(jnp.int32, (16, 128), 1)
    nt = (((1,), (1,)), ((), ()))

    both = jnp.concatenate([t2, td], axis=0)
    prods = widen(lax.dot_general(both, both, nt, precision=HI, preferred_element_type=F32))
    prods = jnp.where(lane < 32, prods[:16], jnp.where(lane < 48, pltpu.roll(prods[16:], 16, 1), 0.0))
    trial1[y * 8 + rad] = pack(prods)
    trial_copies = to_plane(trial1, t1_s, t1_r)

    def locate(j, carry):
        for p in range(16):
            row = stored_ref[partners_ref[j, p]]
            ahead = (row // 64 - z + 16) % 16
            order = jnp.where(ahead > 8, 32 - 2 * ahead, jnp.maximum(2 * ahead - 1, 0))
            place[j * 16 + p] = ((row // 16) % 4 * 16 + order) * 2 + (row // 8) % 2
            place[128 + j * 16 + p] = ((p - row + 16) % 8) * 16
        return carry

    lax.fori_loop(0, NJ, locate, 0)

    sent = []
    for g, (first, end) in enumerate(GROUPS):
        for i in range(first, end):
            if i:
                far[i].wait_recv()
        piece = tbl.at[pl.ds(y * 16 + first, end - first)]
        for k in (2, 1, 3):
            i = g * 3 + k - 1
            sent.append(remote(piece, piece, own_s.at[i], own_r.at[i], at(0, y ^ k)))
    trial2[z] = summed(trial1, trial_copies)
    for c in sent:
        c.wait_recv()
    trial_copies = to_planes(trial2, t2_s, t2_r)

    lane_group = lax.broadcasted_iota(jnp.int32, (16, 128), 1) // 16

    def select(j, carry):
        for hp in range(2):
            acc = jnp.zeros((16, 128), F32)
            for g in range(8):
                i = j * 16 + hp * 8 + g
                moved = pltpu.roll(tbl[place[i] // 2, place[i] % 2].astype(F32), place[128 + i], 1)
                acc = jnp.where(lane_group == g, moved, acc)
            yall[j, rad, :, hp * 128:(hp + 1) * 128] = acc.astype(BF16)
        return carry

    other = (chan, rad ^ 1)
    along_x, across = {}, {}
    n_chunks = NJ // CHUNK
    for c in range(n_chunks):
        lax.fori_loop(c * CHUNK, (c + 1) * CHUNK, select, 0)
        piece = yall.at[pl.ds(c * CHUNK, CHUNK), pl.ds(rad, 1)]
        for i in (2, 1, 3):
            k = c * 3 + i - 1
            along_x[c, i] = remote(piece, piece, x_s.at[k], x_r.at[k], (chan, rad ^ (2 * i)))
        across[c, 0] = remote(piece, piece, c_s.at[c * 4], c_r.at[c * 4], other)

    out_group = lax.broadcasted_iota(jnp.int32, (16, 256), 1) // 16
    applied_r = jnp.zeros((16, 256), F32)
    for c in range(n_chunks + 1):
        if c < n_chunks:
            for i in (1, 3, 2):
                along_x[c, i].wait_recv()
                piece = yall.at[pl.ds(c * CHUNK, CHUNK), pl.ds(rad ^ (2 * i), 1)]
                across[c, i] = remote(piece, piece, c_s.at[c * 4 + i], c_r.at[c * 4 + i], other)
        if c:
            for i in range(4):
                across[c - 1, i].wait_recv()
            js = range((c - 1) * CHUNK, c * CHUNK)
            left = jnp.concatenate([hbuf[:, j].reshape(256, 128) for j in js], axis=1)
            right = yall[(c - 1) * CHUNK:c * CHUNK].reshape(CHUNK * 128, 256)
            out = jnp.dot(left, right, preferred_element_type=F32)
            for p in range(16):
                applied_r += jnp.where(out_group == p, out[p * 16:(p + 1) * 16, :], 0.0)

    turned_a = applied_r.T
    a2 = jnp.concatenate([turned_a[p * 16:(p + 1) * 16, :] for p in range(16)], axis=1)
    ad = a2 / d2

    prods = widen(lax.dot_general(jnp.concatenate([both, ad], axis=0), jnp.concatenate([a2, ad], axis=0), nt,
                                  precision=HI, preferred_element_type=F32))
    prods = jnp.where(lane < 32, prods[:16],
                      jnp.where(lane < 48, pltpu.roll(prods[16:32], 16, 1), pltpu.roll(prods[32:], 32, 1)))
    red1[y * 8 + rad] = pack(prods)
    copies = to_plane(red1, r1_s, r1_r)

    rows = lax.broadcasted_iota(jnp.int32, (16, 128), 0)

    def block(m, b):
        return (pltpu.roll(m, 128 - 16 * b, 1) if b else m)[:, :16]

    trial = unpack(summed(trial2, trial_copies))
    m = jnp.where(lane < 32, trial, jnp.where(lane == rows + 32, 1.0, 0.0))
    for i in range(16):
        pivot_row = m[i:i + 1, :] / m[i:i + 1, i:i + 1]
        m = jnp.where(rows == i, pivot_row, m - m[:, i:i + 1] * pivot_row)
    inv_b, inv_b_ttd = block(m, 2), block(m, 1)
    ttd, tdtd = block(trial, 1), block(trial, 2)

    red2[z] = summed(red1, copies)
    total = unpack(summed(red2, to_planes(red2, r2_s, r2_r)))
    dot = functools.partial(jnp.dot, precision=HI, preferred_element_type=F32)
    solved = dot(inv_b, total)
    coef = block(solved, 0)
    tda = block(total, 2)
    level = dot(jnp.concatenate([ttd, inv_b_ttd, tdtd], axis=0), coef)
    corr = block(total, 1) - level[:16]
    mixing = block(solved, 1) - level[16:32]
    inner = level[32:48] - tda
    tn = (((0,), (0,)), ((), ()))
    gram = block(total, 3) + lax.dot_general(jnp.concatenate([-tda, coef, -corr], axis=0),
                                             jnp.concatenate([coef, inner, mixing], axis=0), tn,
                                             precision=HI, preferred_element_type=F32)
    gram = gram / TOTAL_ROWS
    projected = ad - lax.dot_general(jnp.concatenate([mixing, coef], axis=0), both, tn,
                                     precision=HI, preferred_element_type=F32)
    small = (16, 16)
    diagonal = lax.broadcasted_iota(jnp.int32, small, 0) == lax.broadcasted_iota(jnp.int32, small, 1)
    ritz_ref[...] = jnp.sum(jnp.where(diagonal, coef, 0.0), axis=0, keepdims=True)

    e = jnp.concatenate([gram, jnp.where(diagonal, 1.0, 0.0), jnp.zeros((16, 96), F32)], axis=1)
    for i in range(15):
        e = e - jnp.where(rows > i, e[:, i:i + 1] / e[i:i + 1, i:i + 1], 0.0) * e[i:i + 1, :]
    pivots = jnp.sum(jnp.where(rows == lane, e, 0.0), axis=1, keepdims=True)
    inv_factor = block(e * lax.rsqrt(pivots), 1)
    new = jnp.dot(inv_factor, projected, precision=HI, preferred_element_type=F32)
    for p in range(16):
        half = new[:, (p // 8) * 128:(p // 8 + 1) * 128]
        g = p % 8
        new_ref[p] = (pltpu.roll(half, 128 - 16 * g, 1) if g else half)[:, :16]

    for c in [*far.values(), *sent, *along_x.values(), *across.values(), *sums]:
        c.wait_send()


def body(trial_block, ham_blocks, partners, stored_at, precond_diag):
    vmem = pl.BlockSpec(memory_space=pltpu.VMEM)
    hbm = pl.BlockSpec(memory_space=pltpu.HBM)
    dma = pltpu.SemaphoreType.DMA
    n_chunks = NJ // CHUNK
    counts = (5, 16, 16, 3 * len(GROUPS), 3 * len(GROUPS), 3 * n_chunks, 3 * n_chunks, 4 * n_chunks, 4 * n_chunks, *(31, 31, 16, 16) * 2)
    new_block, ritz = pl.pallas_call(
        kernel,
        out_shape=(jax.ShapeDtypeStruct((16, 16, 16), F32), jax.ShapeDtypeStruct((1, 16), F32)),
        in_specs=[hbm] * 5,
        out_specs=(vmem, vmem),
        scratch_shapes=[
            pltpu.VMEM((16, 16, 16), F32),
            pltpu.VMEM((16, 16), F32),
            pltpu.VMEM((16, 8, 16, 128), BF16),
            pltpu.SMEM((8, 16), jnp.int32),
            pltpu.SMEM((1024,), jnp.int32),
            pltpu.SMEM((256,), jnp.int32),
            pltpu.VMEM((64, 2, 16, 128), BF16),
            pltpu.VMEM((8, 8, 16, 256), BF16),
            *[pltpu.VMEM((n, 8, 128), F32) for n in (32, 16, 32, 16)],
            *[dma((n,)) for n in counts],
        ],
        compiler_params=pltpu.CompilerParams(collective_id=0, has_side_effects=True, vmem_limit_bytes=60 * 2**20),
    )(trial_block, ham_blocks, partners.T, stored_at, precond_diag)
    return new_block, ritz.reshape(16)


def solution(mesh):
    return jax.shard_map(
        body,
        mesh=mesh,
        in_specs=(
            P("chan", None, "rad"),
            P("chan", None, "rad", None),
            P("chan", None),
            P(),
            P("chan", "rad"),
        ),
        out_specs=(P("chan", None, "rad"), P()),
        check_vma=False,
    )
```

```python
import functools

import jax
import jax.numpy as jnp
from jax import lax
from jax.experimental import pallas as pl
from jax.experimental.pallas import tpu as pltpu
from jax.sharding import PartitionSpec as P

MESH = pl.DeviceIdType.MESH
HI = lax.Precision.HIGHEST
F32 = jnp.float32
BF16 = jnp.bfloat16
TOTAL_ROWS = 1024.0 * 128.0
NJ = 8
ALONG_Z = (8, 7, 9, 6, 10, 5, 11, 4, 12, 3, 13, 2, 14, 1, 15)
MIXED_Z = (1, 15, 2, 8, 7, 9, 14, 3, 13, 4, 6, 10, 5, 11, 12)
IN_PLANE = sorted(((dy, dr) for dy in range(4) for dr in range(8) if dy or dr),
                  key=lambda d: -((0, 1, 2, 1)[d[0]] + (0, 1, 2, 1)[d[1] // 2]))
GROUPS = ((0, 4), (4, 8), (8, 12), (12, 16))
CHUNK = 4


def by_distance(d):
    return 2 * d - 1 if 0 < d <= 8 else 2 * (16 - d) % 32


def kernel(t_hbm, ham_hbm, partners_hbm, stored_hbm, d_hbm, new_ref, ritz_ref,
           t_ref, d_ref, hbuf, partners_ref, stored_ref, place, tbl, yall, trial1, trial2, trial3, red1, red2,
           in_sem, far_s, far_r, own_s, own_r, x_s, x_r, c_s, c_r,
           t1_s, t1_r, t2_s, t2_r, t3_s, t3_r, r1_s, r1_r, r2_s, r2_r):
    chan = lax.axis_index("chan")
    rad = lax.axis_index("rad")
    z, y = chan // 4, chan % 4

    def at(dz, yy):
        return (((z + dz + 16) % 16) * 4 + yy, rad)

    t_copy = pltpu.make_async_copy(t_hbm, t_ref, in_sem.at[0])
    t_copy.start()
    barrier = pltpu.get_barrier_semaphore()
    for m in ALONG_Z:
        pl.semaphore_signal(barrier, inc=1, device_id=at(m, y), device_id_type=MESH)
    for k in (2, 1, 3):
        pl.semaphore_signal(barrier, inc=1, device_id=at(0, y ^ k), device_id_type=MESH)
    for i in range(1, 8):
        pl.semaphore_signal(barrier, inc=1, device_id=(chan, rad ^ i), device_id_type=MESH)
    rest = [pltpu.make_async_copy(src, dst, in_sem.at[i + 1]) for i, (src, dst) in enumerate(
        ((d_hbm, d_ref), (partners_hbm, partners_ref), (stored_hbm, stored_ref), (ham_hbm, hbuf)))]
    for c in rest:
        c.start()

    t_copy.wait()
    t2d = t_ref[...].reshape(256, 16)
    eye = (lax.broadcasted_iota(jnp.int32, (16, 16), 0) == lax.broadcasted_iota(jnp.int32, (16, 16), 1)).astype(BF16)
    turned = lax.dot_general(eye, t2d.astype(BF16), (((1,), (1,)), ((), ())), preferred_element_type=F32).astype(BF16)
    tbl[y * 16, 0] = turned[:, :128]
    tbl[y * 16, 1] = turned[:, 128:]

    pl.semaphore_wait(barrier, len(ALONG_Z) + 3 + 7)

    def remote(src, dst, s, r, dev):
        copy = pltpu.make_async_remote_copy(src_ref=src, dst_ref=dst, send_sem=s, recv_sem=r,
                                            device_id=dev, device_id_type=MESH)
        copy.start()
        return copy

    far = {}
    for m in MIXED_Z:
        far[by_distance(16 - m)] = remote(tbl.at[pl.ds(y * 16, 1)], tbl.at[pl.ds(y * 16 + by_distance(16 - m), 1)],
                                          far_s.at[m], far_r.at[m], at(m, y))

    for c in rest:
        c.wait()
    t2 = jnp.concatenate([t_ref[p] for p in range(16)], axis=1)
    d2 = jnp.concatenate([d_ref[p:p + 1, :] for p in range(16)], axis=1)
    td = t2 / d2

    def pack(m):
        left_half = lax.broadcasted_iota(jnp.int32, (8, 128), 1) < 64
        return jnp.where(left_half, m[:8], pltpu.roll(m[8:], 64, 1))

    def unpack(m):
        return jnp.concatenate([m, pltpu.roll(m, 64, 1)], axis=0)

    def widen(m):
        return jnp.concatenate([m, jnp.zeros((m.shape[0], 128 - m.shape[1]), F32)], axis=1)

    sums = []

    def to_plane(buf, s, r):
        piece = buf.at[pl.ds(y * 8 + rad, 1)]
        return [remote(piece, piece, s.at[i], r.at[i], (z * 4 + (y ^ dy), rad ^ dr))
                for i, (dy, dr) in enumerate(IN_PLANE)]

    def to_rad(buf, s, r):
        piece = buf.at[pl.ds(rad, 1)]
        return [remote(piece, piece, s.at[i - 1], r.at[i - 1], (chan, rad ^ i)) for i in range(1, 8)]

    def to_y(buf, s, r):
        piece = buf.at[pl.ds(y, 1)]
        return [remote(piece, piece, s.at[k - 1], r.at[k - 1], at(0, y ^ k)) for k in (2, 1, 3)]

    def to_planes(buf, s, r):
        piece = buf.at[pl.ds(z, 1)]
        return [remote(piece, piece, s.at[m], r.at[m], at(m, y)) for m in ALONG_Z]

    def summed(buf, copies):
        for c in copies:
            c.wait_recv()
        sums.extend(copies)
        parts = [buf[i] for i in range(buf.shape[0])]
        while len(parts) > 1:
            parts = [u + v for u, v in zip(parts[::2], parts[1::2])]
        return parts[0]

    lane = lax.broadcasted_iota(jnp.int32, (16, 128), 1)
    nt = (((1,), (1,)), ((), ()))

    both = jnp.concatenate([t2, td], axis=0)
    prods = widen(lax.dot_general(both, both, nt, precision=HI, preferred_element_type=F32))
    prods = jnp.where(lane < 32, prods[:16], jnp.where(lane < 48, pltpu.roll(prods[16:], 16, 1), 0.0))
    trial1[rad] = pack(prods)
    trial_copies = to_rad(trial1, t1_s, t1_r)

    def locate(j, carry):
        for p in range(16):
            row = stored_ref[partners_ref[j, p]]
            ahead = (row // 64 - z + 16) % 16
            order = jnp.where(ahead > 8, 32 - 2 * ahead, jnp.maximum(2 * ahead - 1, 0))
            place[j * 16 + p] = ((row // 16) % 4 * 16 + order) * 2 + (row // 8) % 2
            place[128 + j * 16 + p] = ((p - row + 16) % 8) * 16
        return carry

    lax.fori_loop(0, NJ, locate, 0)

    sent = []
    for g, (first, end) in enumerate(GROUPS):
        for i in range(first, end):
            if i:
                far[i].wait_recv()
        piece = tbl.at[pl.ds(y * 16 + first, end - first)]
        for k in (2, 1, 3):
            i = g * 3 + k - 1
            sent.append(remote(piece, piece, own_s.at[i], own_r.at[i], at(0, y ^ k)))
    trial2[y] = summed(trial1, trial_copies)
    trial_copies = to_y(trial2, t2_s, t2_r)
    for c in sent:
        c.wait_recv()

    lane_group = lax.broadcasted_iota(jnp.int32, (16, 128), 1) // 16

    def select(j, carry):
        for hp in range(2):
            acc = jnp.zeros((16, 128), F32)
            for g in range(8):
                i = j * 16 + hp * 8 + g
                moved = pltpu.roll(tbl[place[i] // 2, place[i] % 2].astype(F32), place[128 + i], 1)
                acc = jnp.where(lane_group == g, moved, acc)
            yall[j, rad, :, hp * 128:(hp + 1) * 128] = acc.astype(BF16)
        return carry

    other = (chan, rad ^ 1)
    along_x, across = {}, {}
    n_chunks = NJ // CHUNK
    for c in range(n_chunks):
        lax.fori_loop(c * CHUNK, (c + 1) * CHUNK, select, 0)
        piece = yall.at[pl.ds(c * CHUNK, CHUNK), pl.ds(rad, 1)]
        for i in (2, 1, 3):
            k = c * 3 + i - 1
            along_x[c, i] = remote(piece, piece, x_s.at[k], x_r.at[k], (chan, rad ^ (2 * i)))
        across[c, 0] = remote(piece, piece, c_s.at[c * 4], c_r.at[c * 4], other)

    trial3[z] = summed(trial2, trial_copies)
    trial_copies = to_planes(trial3, t3_s, t3_r)
    out_group = lax.broadcasted_iota(jnp.int32, (16, 256), 1) // 16
    applied_r = jnp.zeros((16, 256), F32)
    for c in range(n_chunks + 1):
        if c < n_chunks:
            for i in (1, 3, 2):
                along_x[c, i].wait_recv()
                piece = yall.at[pl.ds(c * CHUNK, CHUNK), pl.ds(rad ^ (2 * i), 1)]
                across[c, i] = remote(piece, piece, c_s.at[c * 4 + i], c_r.at[c * 4 + i], other)
        if c:
            for i in range(4):
                across[c - 1, i].wait_recv()
            js = range((c - 1) * CHUNK, c * CHUNK)
            left = jnp.concatenate([hbuf[:, j].reshape(256, 128) for j in js], axis=1)
            right = yall[(c - 1) * CHUNK:c * CHUNK].reshape(CHUNK * 128, 256)
            out = jnp.dot(left, right, preferred_element_type=F32)
            for p in range(16):
                applied_r += jnp.where(out_group == p, out[p * 16:(p + 1) * 16, :], 0.0)

    turned_a = applied_r.T
    a2 = jnp.concatenate([turned_a[p * 16:(p + 1) * 16, :] for p in range(16)], axis=1)
    ad = a2 / d2

    prods = widen(lax.dot_general(jnp.concatenate([both, ad], axis=0), jnp.concatenate([a2, ad], axis=0), nt,
                                  precision=HI, preferred_element_type=F32))
    prods = jnp.where(lane < 32, prods[:16],
                      jnp.where(lane < 48, pltpu.roll(prods[16:32], 16, 1), pltpu.roll(prods[32:], 32, 1)))
    red1[y * 8 + rad] = pack(prods)
    copies = to_plane(red1, r1_s, r1_r)

    rows = lax.broadcasted_iota(jnp.int32, (16, 128), 0)

    def block(m, b):
        return (pltpu.roll(m, 128 - 16 * b, 1) if b else m)[:, :16]

    trial = unpack(summed(trial3, trial_copies))
    m = jnp.where(lane < 32, trial, jnp.where(lane == rows + 32, 1.0, 0.0))
    for i in range(16):
        pivot_row = m[i:i + 1, :] / m[i:i + 1, i:i + 1]
        m = jnp.where(rows == i, pivot_row, m - m[:, i:i + 1] * pivot_row)
    inv_b, inv_b_ttd = block(m, 2), block(m, 1)
    ttd, tdtd = block(trial, 1), block(trial, 2)

    red2[z] = summed(red1, copies)
    total = unpack(summed(red2, to_planes(red2, r2_s, r2_r)))
    dot = functools.partial(jnp.dot, precision=HI, preferred_element_type=F32)
    solved = dot(inv_b, total)
    coef = block(solved, 0)
    tda = block(total, 2)
    level = dot(jnp.concatenate([ttd, inv_b_ttd, tdtd], axis=0), coef)
    corr = block(total, 1) - level[:16]
    mixing = block(solved, 1) - level[16:32]
    inner = level[32:48] - tda
    tn = (((0,), (0,)), ((), ()))
    gram = block(total, 3) + lax.dot_general(jnp.concatenate([-tda, coef, -corr], axis=0),
                                             jnp.concatenate([coef, inner, mixing], axis=0), tn,
                                             precision=HI, preferred_element_type=F32)
    gram = gram / TOTAL_ROWS
    projected = ad - lax.dot_general(jnp.concatenate([mixing, coef], axis=0), both, tn,
                                     precision=HI, preferred_element_type=F32)
    small = (16, 16)
    diagonal = lax.broadcasted_iota(jnp.int32, small, 0) == lax.broadcasted_iota(jnp.int32, small, 1)
    ritz_ref[...] = jnp.sum(jnp.where(diagonal, coef, 0.0), axis=0, keepdims=True)

    e = jnp.concatenate([gram, jnp.where(diagonal, 1.0, 0.0), jnp.zeros((16, 96), F32)], axis=1)
    for i in range(15):
        e = e - jnp.where(rows > i, e[:, i:i + 1] / e[i:i + 1, i:i + 1], 0.0) * e[i:i + 1, :]
    pivots = jnp.sum(jnp.where(rows == lane, e, 0.0), axis=1, keepdims=True)
    inv_factor = block(e * lax.rsqrt(pivots), 1)
    new = jnp.dot(inv_factor, projected, precision=HI, preferred_element_type=F32)
    for p in range(16):
        half = new[:, (p // 8) * 128:(p // 8 + 1) * 128]
        g = p % 8
        new_ref[p] = (pltpu.roll(half, 128 - 16 * g, 1) if g else half)[:, :16]

    for c in [*far.values(), *sent, *along_x.values(), *across.values(), *sums]:
        c.wait_send()


def body(trial_block, ham_blocks, partners, stored_at, precond_diag):
    vmem = pl.BlockSpec(memory_space=pltpu.VMEM)
    hbm = pl.BlockSpec(memory_space=pltpu.HBM)
    dma = pltpu.SemaphoreType.DMA
    n_chunks = NJ // CHUNK
    counts = (5, 16, 16, 3 * len(GROUPS), 3 * len(GROUPS), 3 * n_chunks, 3 * n_chunks, 4 * n_chunks, 4 * n_chunks, 7, 7, 3, 3, 16, 16, 31, 31, 16, 16)
    new_block, ritz = pl.pallas_call(
        kernel,
        out_shape=(jax.ShapeDtypeStruct((16, 16, 16), F32), jax.ShapeDtypeStruct((1, 16), F32)),
        in_specs=[hbm] * 5,
        out_specs=(vmem, vmem),
        scratch_shapes=[
            pltpu.VMEM((16, 16, 16), F32),
            pltpu.VMEM((16, 16), F32),
            pltpu.VMEM((16, 8, 16, 128), BF16),
            pltpu.SMEM((8, 16), jnp.int32),
            pltpu.SMEM((1024,), jnp.int32),
            pltpu.SMEM((256,), jnp.int32),
            pltpu.VMEM((64, 2, 16, 128), BF16),
            pltpu.VMEM((8, 8, 16, 256), BF16),
            *[pltpu.VMEM((n, 8, 128), F32) for n in (8, 4, 16, 32, 16)],
            *[dma((n,)) for n in counts],
        ],
        compiler_params=pltpu.CompilerParams(collective_id=0, has_side_effects=True, vmem_limit_bytes=60 * 2**20),
    )(trial_block, ham_blocks, partners.T, stored_at, precond_diag)
    return new_block, ritz.reshape(16)


def solution(mesh):
    return jax.shard_map(
        body,
        mesh=mesh,
        in_specs=(
            P("chan", None, "rad"),
            P("chan", None, "rad", None),
            P("chan", None),
            P(),
            P("chan", "rad"),
        ),
        out_specs=(P("chan", None, "rad"), P()),
        check_vma=False,
    )
```

```python
import functools

import jax
import jax.numpy as jnp
from jax import lax
from jax.experimental import pallas as pl
from jax.experimental.pallas import tpu as pltpu
from jax.sharding import PartitionSpec as P

MESH = pl.DeviceIdType.MESH
HI = lax.Precision.HIGHEST
F32 = jnp.float32
BF16 = jnp.bfloat16
TOTAL_ROWS = 1024.0 * 128.0
NJ = 8
NEAR_Z = (4, 12, 3, 13, 2, 14, 1, 15)
ALONG_Z = (8, 7, 9, 6, 10, 5, 11, 4, 12, 3, 13, 2, 14, 1, 15)
IN_PLANE = sorted(((dy, dr) for dy in range(4) for dr in range(8) if dy or dr),
                  key=lambda d: -((0, 1, 2, 1)[d[0]] + (0, 1, 2, 1)[d[1] // 2]))
CHUNK = 4


def kernel(t_hbm, ham_hbm, partners_hbm, stored_hbm, d_hbm, new_ref, ritz_ref,
           t_ref, d_ref, hbuf, partners_ref, stored_ref, place, tbl, yall, trial1, trial2, trial3, red1, red2,
           in_sem, far_s, far_r, own_s, own_r, x_s, x_r, c_s, c_r,
           t1_s, t1_r, t2_s, t2_r, t3_s, t3_r, r1_s, r1_r, r2_s, r2_r):
    chan = lax.axis_index("chan")
    rad = lax.axis_index("rad")
    z, y = chan // 4, chan % 4

    def at(dz, yy):
        return (((z + dz + 16) % 16) * 4 + yy, rad)

    t_copy = pltpu.make_async_copy(t_hbm, t_ref, in_sem.at[0])
    t_copy.start()
    barrier = pltpu.get_barrier_semaphore()
    for m in NEAR_Z:
        pl.semaphore_signal(barrier, inc=1, device_id=at(m, y), device_id_type=MESH)
    for k in (2, 1, 3):
        pl.semaphore_signal(barrier, inc=1, device_id=at(0, y ^ k), device_id_type=MESH)
    for i in range(1, 8):
        pl.semaphore_signal(barrier, inc=1, device_id=(chan, rad ^ i), device_id_type=MESH)
    rest = [pltpu.make_async_copy(src, dst, in_sem.at[i + 1]) for i, (src, dst) in enumerate(
        ((d_hbm, d_ref), (partners_hbm, partners_ref), (stored_hbm, stored_ref), (ham_hbm, hbuf)))]
    for c in rest:
        c.start()

    t_copy.wait()
    t2d = t_ref[...].reshape(256, 16)
    eye = (lax.broadcasted_iota(jnp.int32, (16, 16), 0) == lax.broadcasted_iota(jnp.int32, (16, 16), 1)).astype(BF16)
    turned = lax.dot_general(eye, t2d.astype(BF16), (((1,), (1,)), ((), ())), preferred_element_type=F32).astype(BF16)
    tbl[y * 16, 0] = turned[:, :128]
    tbl[y * 16, 1] = turned[:, 128:]

    pl.semaphore_wait(barrier, len(NEAR_Z) + 3 + 7)

    def remote(src, dst, s, r, dev):
        copy = pltpu.make_async_remote_copy(src_ref=src, dst_ref=dst, send_sem=s, recv_sem=r,
                                            device_id=dev, device_id_type=MESH)
        copy.start()
        return copy

    def blocks(first, end):
        return tbl.at[pl.ds(y * 16 + first, end - first)]

    far = {}
    for m in NEAR_Z:
        far[16 - m] = remote(blocks(0, 1), blocks(16 - m, 17 - m), far_s.at[m], far_r.at[m], at(m, y))

    for c in rest:
        c.wait()
    t2 = jnp.concatenate([t_ref[p] for p in range(16)], axis=1)
    d2 = jnp.concatenate([d_ref[p:p + 1, :] for p in range(16)], axis=1)
    td = t2 / d2

    def pack(m):
        left_half = lax.broadcasted_iota(jnp.int32, (8, 128), 1) < 64
        return jnp.where(left_half, m[:8], pltpu.roll(m[8:], 64, 1))

    def unpack(m):
        return jnp.concatenate([m, pltpu.roll(m, 64, 1)], axis=0)

    def widen(m):
        return jnp.concatenate([m, jnp.zeros((m.shape[0], 128 - m.shape[1]), F32)], axis=1)

    sums = []

    def to_plane(buf, s, r):
        piece = buf.at[pl.ds(y * 8 + rad, 1)]
        return [remote(piece, piece, s.at[i], r.at[i], (z * 4 + (y ^ dy), rad ^ dr))
                for i, (dy, dr) in enumerate(IN_PLANE)]

    def to_rad(buf, s, r):
        piece = buf.at[pl.ds(rad, 1)]
        return [remote(piece, piece, s.at[i - 1], r.at[i - 1], (chan, rad ^ i)) for i in range(1, 8)]

    def to_y(buf, s, r):
        piece = buf.at[pl.ds(y, 1)]
        return [remote(piece, piece, s.at[k - 1], r.at[k - 1], at(0, y ^ k)) for k in (2, 1, 3)]

    def to_planes(buf, s, r):
        piece = buf.at[pl.ds(z, 1)]
        return [remote(piece, piece, s.at[m], r.at[m], at(m, y)) for m in ALONG_Z]

    def summed(buf, copies):
        for c in copies:
            c.wait_recv()
        sums.extend(copies)
        parts = [buf[i] for i in range(buf.shape[0])]
        while len(parts) > 1:
            parts = [u + v for u, v in zip(parts[::2], parts[1::2])]
        return parts[0]

    lane = lax.broadcasted_iota(jnp.int32, (16, 128), 1)
    nt = (((1,), (1,)), ((), ()))

    both = jnp.concatenate([t2, td], axis=0)
    prods = widen(lax.dot_general(both, both, nt, precision=HI, preferred_element_type=F32))
    prods = jnp.where(lane < 32, prods[:16], jnp.where(lane < 48, pltpu.roll(prods[16:], 16, 1), 0.0))
    trial1[rad] = pack(prods)
    trial_copies = to_rad(trial1, t1_s, t1_r)

    def locate(j, carry):
        for p in range(16):
            row = stored_ref[partners_ref[j, p]]
            ahead = (row // 64 - z + 16) % 16
            place[j * 16 + p] = ((row // 16) % 4 * 16 + ahead) * 2 + (row // 8) % 2
            place[128 + j * 16 + p] = ((p - row + 16) % 8) * 16
        return carry

    lax.fori_loop(0, NJ, locate, 0)

    sent, passed = [], []

    def along_y(first, end, g):
        for k in (2, 1, 3):
            i = g * 3 + k - 1
            sent.append(remote(blocks(first, end), blocks(first, end), own_s.at[i], own_r.at[i], at(0, y ^ k)))

    for i in (13, 14, 15):
        far[i].wait_recv()
    passed.append(remote(blocks(13, 16), blocks(9, 12), far_s.at[5], far_r.at[5], at(4, y)))
    for i in (1, 2, 3, 4):
        far[i].wait_recv()
    passed.append(remote(blocks(1, 5), blocks(5, 9), far_s.at[6], far_r.at[6], at(-4, y)))
    along_y(0, 5, 0)
    far[12].wait_recv()
    along_y(12, 16, 1)
    trial2[y] = summed(trial1, trial_copies)
    trial_copies = to_y(trial2, t2_s, t2_r)
    passed[0].wait_recv()
    along_y(9, 12, 2)
    passed[1].wait_recv()
    along_y(5, 9, 3)
    for c in sent:
        c.wait_recv()

    lane_group = lax.broadcasted_iota(jnp.int32, (16, 128), 1) // 16

    def select(j, carry):
        for hp in range(2):
            acc = jnp.zeros((16, 128), F32)
            for g in range(8):
                i = j * 16 + hp * 8 + g
                moved = pltpu.roll(tbl[place[i] // 2, place[i] % 2].astype(F32), place[128 + i], 1)
                acc = jnp.where(lane_group == g, moved, acc)
            yall[j, rad, :, hp * 128:(hp + 1) * 128] = acc.astype(BF16)
        return carry

    other = (chan, rad ^ 1)
    along_x, across = {}, {}
    n_chunks = NJ // CHUNK
    for c in range(n_chunks):
        lax.fori_loop(c * CHUNK, (c + 1) * CHUNK, select, 0)
        piece = yall.at[pl.ds(c * CHUNK, CHUNK), pl.ds(rad, 1)]
        for i in (2, 1, 3):
            k = c * 3 + i - 1
            along_x[c, i] = remote(piece, piece, x_s.at[k], x_r.at[k], (chan, rad ^ (2 * i)))
        across[c, 0] = remote(piece, piece, c_s.at[c * 4], c_r.at[c * 4], other)

    trial3[z] = summed(trial2, trial_copies)
    trial_copies = to_planes(trial3, t3_s, t3_r)
    out_group = lax.broadcasted_iota(jnp.int32, (16, 256), 1) // 16
    applied_r = jnp.zeros((16, 256), F32)
    for c in range(n_chunks + 1):
        if c < n_chunks:
            for i in (1, 3, 2):
                along_x[c, i].wait_recv()
                piece = yall.at[pl.ds(c * CHUNK, CHUNK), pl.ds(rad ^ (2 * i), 1)]
                across[c, i] = remote(piece, piece, c_s.at[c * 4 + i], c_r.at[c * 4 + i], other)
        if c:
            for i in range(4):
                across[c - 1, i].wait_recv()
            js = range((c - 1) * CHUNK, c * CHUNK)
            left = jnp.concatenate([hbuf[:, j].reshape(256, 128) for j in js], axis=1)
            right = yall[(c - 1) * CHUNK:c * CHUNK].reshape(CHUNK * 128, 256)
            out = jnp.dot(left, right, preferred_element_type=F32)
            for p in range(16):
                applied_r += jnp.where(out_group == p, out[p * 16:(p + 1) * 16, :], 0.0)

    turned_a = applied_r.T
    a2 = jnp.concatenate([turned_a[p * 16:(p + 1) * 16, :] for p in range(16)], axis=1)
    ad = a2 / d2

    prods = widen(lax.dot_general(jnp.concatenate([both, ad], axis=0), jnp.concatenate([a2, ad], axis=0), nt,
                                  precision=HI, preferred_element_type=F32))
    prods = jnp.where(lane < 32, prods[:16],
                      jnp.where(lane < 48, pltpu.roll(prods[16:32], 16, 1), pltpu.roll(prods[32:], 32, 1)))
    red1[y * 8 + rad] = pack(prods)
    copies = to_plane(red1, r1_s, r1_r)

    rows = lax.broadcasted_iota(jnp.int32, (16, 128), 0)

    def block(m, b):
        return (pltpu.roll(m, 128 - 16 * b, 1) if b else m)[:, :16]

    trial = unpack(summed(trial3, trial_copies))
    m = jnp.where(lane < 32, trial, jnp.where(lane == rows + 32, 1.0, 0.0))
    for i in range(16):
        pivot_row = m[i:i + 1, :] / m[i:i + 1, i:i + 1]
        m = jnp.where(rows == i, pivot_row, m - m[:, i:i + 1] * pivot_row)
    inv_b, inv_b_ttd = block(m, 2), block(m, 1)
    ttd, tdtd = block(trial, 1), block(trial, 2)

    red2[z] = summed(red1, copies)
    total = unpack(summed(red2, to_planes(red2, r2_s, r2_r)))
    dot = functools.partial(jnp.dot, precision=HI, preferred_element_type=F32)
    solved = dot(inv_b, total)
    coef = block(solved, 0)
    tda = block(total, 2)
    level = dot(jnp.concatenate([ttd, inv_b_ttd, tdtd], axis=0), coef)
    corr = block(total, 1) - level[:16]
    mixing = block(solved, 1) - level[16:32]
    inner = level[32:48] - tda
    tn = (((0,), (0,)), ((), ()))
    gram = block(total, 3) + lax.dot_general(jnp.concatenate([-tda, coef, -corr], axis=0),
                                             jnp.concatenate([coef, inner, mixing], axis=0), tn,
                                             precision=HI, preferred_element_type=F32)
    gram = gram / TOTAL_ROWS
    projected = ad - lax.dot_general(jnp.concatenate([mixing, coef], axis=0), both, tn,
                                     precision=HI, preferred_element_type=F32)
    small = (16, 16)
    diagonal = lax.broadcasted_iota(jnp.int32, small, 0) == lax.broadcasted_iota(jnp.int32, small, 1)
    ritz_ref[...] = jnp.sum(jnp.where(diagonal, coef, 0.0), axis=0, keepdims=True)

    e = jnp.concatenate([gram, jnp.where(diagonal, 1.0, 0.0), jnp.zeros((16, 96), F32)], axis=1)
    for i in range(15):
        e = e - jnp.where(rows > i, e[:, i:i + 1] / e[i:i + 1, i:i + 1], 0.0) * e[i:i + 1, :]
    pivots = jnp.sum(jnp.where(rows == lane, e, 0.0), axis=1, keepdims=True)
    inv_factor = block(e * lax.rsqrt(pivots), 1)
    new = jnp.dot(inv_factor, projected, precision=HI, preferred_element_type=F32)
    for p in range(16):
        half = new[:, (p // 8) * 128:(p // 8 + 1) * 128]
        g = p % 8
        new_ref[p] = (pltpu.roll(half, 128 - 16 * g, 1) if g else half)[:, :16]

    for c in [*far.values(), *passed, *sent, *along_x.values(), *across.values(), *sums]:
        c.wait_send()


def body(trial_block, ham_blocks, partners, stored_at, precond_diag):
    vmem = pl.BlockSpec(memory_space=pltpu.VMEM)
    hbm = pl.BlockSpec(memory_space=pltpu.HBM)
    dma = pltpu.SemaphoreType.DMA
    n_chunks = NJ // CHUNK
    counts = (5, 16, 16, 12, 12, 3 * n_chunks, 3 * n_chunks, 4 * n_chunks, 4 * n_chunks, 7, 7, 3, 3, 16, 16, 31, 31, 16, 16)
    new_block, ritz = pl.pallas_call(
        kernel,
        out_shape=(jax.ShapeDtypeStruct((16, 16, 16), F32), jax.ShapeDtypeStruct((1, 16), F32)),
        in_specs=[hbm] * 5,
        out_specs=(vmem, vmem),
        scratch_shapes=[
            pltpu.VMEM((16, 16, 16), F32),
            pltpu.VMEM((16, 16), F32),
            pltpu.VMEM((16, 8, 16, 128), BF16),
            pltpu.SMEM((8, 16), jnp.int32),
            pltpu.SMEM((1024,), jnp.int32),
            pltpu.SMEM((256,), jnp.int32),
            pltpu.VMEM((64, 2, 16, 128), BF16),
            pltpu.VMEM((8, 8, 16, 256), BF16),
            *[pltpu.VMEM((n, 8, 128), F32) for n in (8, 4, 16, 32, 16)],
            *[dma((n,)) for n in counts],
        ],
        compiler_params=pltpu.CompilerParams(collective_id=0, has_side_effects=True, vmem_limit_bytes=60 * 2**20),
    )(trial_block, ham_blocks, partners.T, stored_at, precond_diag)
    return new_block, ritz.reshape(16)


def solution(mesh):
    return jax.shard_map(
        body,
        mesh=mesh,
        in_specs=(
            P("chan", None, "rad"),
            P("chan", None, "rad", None),
            P("chan", None),
            P(),
            P("chan", "rad"),
        ),
        out_specs=(P("chan", None, "rad"), P()),
        check_vma=False,
    )
```

```python
import functools

import jax
import jax.numpy as jnp
from jax import lax
from jax.experimental import pallas as pl
from jax.experimental.pallas import tpu as pltpu
from jax.sharding import PartitionSpec as P

MESH = pl.DeviceIdType.MESH
HI = lax.Precision.HIGHEST
F32 = jnp.float32
BF16 = jnp.bfloat16
TOTAL_ROWS = 1024.0 * 128.0
NJ = 8
NEAR_Z = (4, 12, 3, 13, 2, 14, 1, 15)
ALONG_Z = (8, 7, 9, 6, 10, 5, 11, 4, 12, 3, 13, 2, 14, 1, 15)
IN_PLANE = sorted(((dy, dr) for dy in range(4) for dr in range(8) if dy or dr),
                  key=lambda d: -((0, 1, 2, 1)[d[0]] + (0, 1, 2, 1)[d[1] // 2]))
CHUNK = 4


def kernel(t_hbm, ham_hbm, partners_hbm, stored_hbm, d_hbm, total_ref, inverse_ref, trial_ref, states_ref,
           t_ref, d_ref, hbuf, partners_ref, stored_ref, place, tbl, yall, trial1, trial2, trial3, red1, red2,
           in_sem, far_s, far_r, own_s, own_r, x_s, x_r, c_s, c_r,
           t1_s, t1_r, t2_s, t2_r, t3_s, t3_r, r1_s, r1_r, r2_s, r2_r):
    chan = lax.axis_index("chan")
    rad = lax.axis_index("rad")
    z, y = chan // 4, chan % 4

    def at(dz, yy):
        return (((z + dz + 16) % 16) * 4 + yy, rad)

    t_copy = pltpu.make_async_copy(t_hbm, t_ref, in_sem.at[0])
    t_copy.start()
    barrier = pltpu.get_barrier_semaphore()
    for m in NEAR_Z:
        pl.semaphore_signal(barrier, inc=1, device_id=at(m, y), device_id_type=MESH)
    for k in (2, 1, 3):
        pl.semaphore_signal(barrier, inc=1, device_id=at(0, y ^ k), device_id_type=MESH)
    for i in range(1, 8):
        pl.semaphore_signal(barrier, inc=1, device_id=(chan, rad ^ i), device_id_type=MESH)
    rest = [pltpu.make_async_copy(src, dst, in_sem.at[i + 1]) for i, (src, dst) in enumerate(
        ((d_hbm, d_ref), (partners_hbm, partners_ref), (stored_hbm, stored_ref), (ham_hbm, hbuf)))]
    for c in rest:
        c.start()

    t_copy.wait()
    t2d = t_ref[...].reshape(256, 16)
    eye = (lax.broadcasted_iota(jnp.int32, (16, 16), 0) == lax.broadcasted_iota(jnp.int32, (16, 16), 1)).astype(BF16)
    turned = lax.dot_general(eye, t2d.astype(BF16), (((1,), (1,)), ((), ())), preferred_element_type=F32).astype(BF16)
    tbl[y * 16, 0] = turned[:, :128]
    tbl[y * 16, 1] = turned[:, 128:]

    pl.semaphore_wait(barrier, len(NEAR_Z) + 3 + 7)

    def remote(src, dst, s, r, dev):
        copy = pltpu.make_async_remote_copy(src_ref=src, dst_ref=dst, send_sem=s, recv_sem=r,
                                            device_id=dev, device_id_type=MESH)
        copy.start()
        return copy

    def blocks(first, end):
        return tbl.at[pl.ds(y * 16 + first, end - first)]

    far = {}
    for m in NEAR_Z:
        far[16 - m] = remote(blocks(0, 1), blocks(16 - m, 17 - m), far_s.at[m], far_r.at[m], at(m, y))

    for c in rest:
        c.wait()
    t2 = jnp.concatenate([t_ref[p] for p in range(16)], axis=1)
    d2 = jnp.concatenate([d_ref[p:p + 1, :] for p in range(16)], axis=1)
    td = t2 / d2

    def pack(m):
        left_half = lax.broadcasted_iota(jnp.int32, (8, 128), 1) < 64
        return jnp.where(left_half, m[:8], pltpu.roll(m[8:], 64, 1))

    def unpack(m):
        return jnp.concatenate([m, pltpu.roll(m, 64, 1)], axis=0)

    def widen(m):
        return jnp.concatenate([m, jnp.zeros((m.shape[0], 128 - m.shape[1]), F32)], axis=1)

    sums = []

    def to_plane(buf, s, r):
        piece = buf.at[pl.ds(y * 8 + rad, 1)]
        return [remote(piece, piece, s.at[i], r.at[i], (z * 4 + (y ^ dy), rad ^ dr))
                for i, (dy, dr) in enumerate(IN_PLANE)]

    def to_rad(buf, s, r):
        piece = buf.at[pl.ds(rad, 1)]
        return [remote(piece, piece, s.at[i - 1], r.at[i - 1], (chan, rad ^ i)) for i in range(1, 8)]

    def to_y(buf, s, r):
        piece = buf.at[pl.ds(y, 1)]
        return [remote(piece, piece, s.at[k - 1], r.at[k - 1], at(0, y ^ k)) for k in (2, 1, 3)]

    def to_planes(buf, s, r):
        piece = buf.at[pl.ds(z, 1)]
        return [remote(piece, piece, s.at[m], r.at[m], at(m, y)) for m in ALONG_Z]

    def summed(buf, copies):
        for c in copies:
            c.wait_recv()
        sums.extend(copies)
        parts = [buf[i] for i in range(buf.shape[0])]
        while len(parts) > 1:
            parts = [u + v for u, v in zip(parts[::2], parts[1::2])]
        return parts[0]

    lane = lax.broadcasted_iota(jnp.int32, (16, 128), 1)
    nt = (((1,), (1,)), ((), ()))

    both = jnp.concatenate([t2, td], axis=0)
    prods = widen(lax.dot_general(both, both, nt, precision=HI, preferred_element_type=F32))
    prods = jnp.where(lane < 32, prods[:16], jnp.where(lane < 48, pltpu.roll(prods[16:], 16, 1), 0.0))
    trial1[rad] = pack(prods)
    trial_copies = to_rad(trial1, t1_s, t1_r)

    def locate(j, carry):
        for p in range(16):
            row = stored_ref[partners_ref[j, p]]
            ahead = (row // 64 - z + 16) % 16
            place[j * 16 + p] = ((row // 16) % 4 * 16 + ahead) * 2 + (row // 8) % 2
            place[128 + j * 16 + p] = ((p - row + 16) % 8) * 16
        return carry

    lax.fori_loop(0, NJ, locate, 0)

    sent, passed = [], []

    def along_y(first, end, g):
        for k in (2, 1, 3):
            i = g * 3 + k - 1
            sent.append(remote(blocks(first, end), blocks(first, end), own_s.at[i], own_r.at[i], at(0, y ^ k)))

    for n, (take, first, end, to, dz) in enumerate((
            ((15, 14), 14, 16, 10, 4), ((1, 2), 1, 3, 5, -4), ((13,), 13, 14, 9, 4), ((3, 4), 3, 5, 7, -4))):
        for i in take:
            far[i].wait_recv()
        passed.append(remote(blocks(first, end), blocks(to, to + end - first), far_s.at[5 + n], far_r.at[5 + n], at(dz, y)))
    along_y(0, 5, 0)
    far[12].wait_recv()
    along_y(12, 16, 1)
    trial2[y] = summed(trial1, trial_copies)
    trial_copies = to_y(trial2, t2_s, t2_r)
    for n, (first, end) in enumerate(((10, 12), (5, 7), (9, 10), (7, 9))):
        passed[n].wait_recv()
        along_y(first, end, 2 + n)
    for c in sent:
        c.wait_recv()

    lane_group = lax.broadcasted_iota(jnp.int32, (16, 128), 1) // 16

    def select(j, carry):
        for hp in range(2):
            acc = jnp.zeros((16, 128), F32)
            for g in range(8):
                i = j * 16 + hp * 8 + g
                moved = pltpu.roll(tbl[place[i] // 2, place[i] % 2].astype(F32), place[128 + i], 1)
                acc = jnp.where(lane_group == g, moved, acc)
            yall[j, rad, :, hp * 128:(hp + 1) * 128] = acc.astype(BF16)
        return carry

    other = (chan, rad ^ 1)
    along_x, across = {}, {}
    n_chunks = NJ // CHUNK
    for c in range(n_chunks):
        lax.fori_loop(c * CHUNK, (c + 1) * CHUNK, select, 0)
        piece = yall.at[pl.ds(c * CHUNK, CHUNK), pl.ds(rad, 1)]
        for i in (2, 1, 3):
            k = c * 3 + i - 1
            along_x[c, i] = remote(piece, piece, x_s.at[k], x_r.at[k], (chan, rad ^ (2 * i)))
        across[c, 0] = remote(piece, piece, c_s.at[c * 4], c_r.at[c * 4], other)

    trial3[z] = summed(trial2, trial_copies)
    trial_copies = to_planes(trial3, t3_s, t3_r)
    out_group = lax.broadcasted_iota(jnp.int32, (16, 256), 1) // 16
    applied_r = jnp.zeros((16, 256), F32)
    for c in range(n_chunks + 1):
        if c < n_chunks:
            for i in (1, 3, 2):
                along_x[c, i].wait_recv()
                piece = yall.at[pl.ds(c * CHUNK, CHUNK), pl.ds(rad ^ (2 * i), 1)]
                across[c, i] = remote(piece, piece, c_s.at[c * 4 + i], c_r.at[c * 4 + i], other)
        if c:
            for i in range(4):
                across[c - 1, i].wait_recv()
            js = range((c - 1) * CHUNK, c * CHUNK)
            left = jnp.concatenate([hbuf[:, j].reshape(256, 128) for j in js], axis=1)
            right = yall[(c - 1) * CHUNK:c * CHUNK].reshape(CHUNK * 128, 256)
            out = jnp.dot(left, right, preferred_element_type=F32)
            for p in range(16):
                applied_r += jnp.where(out_group == p, out[p * 16:(p + 1) * 16, :], 0.0)

    turned_a = applied_r.T
    a2 = jnp.concatenate([turned_a[p * 16:(p + 1) * 16, :] for p in range(16)], axis=1)
    ad = a2 / d2

    prods = widen(lax.dot_general(jnp.concatenate([both, ad], axis=0), jnp.concatenate([a2, ad], axis=0), nt,
                                  precision=HI, preferred_element_type=F32))
    prods = jnp.where(lane < 32, prods[:16],
                      jnp.where(lane < 48, pltpu.roll(prods[16:32], 16, 1), pltpu.roll(prods[32:], 32, 1)))
    red1[y * 8 + rad] = pack(prods)
    copies = to_plane(red1, r1_s, r1_r)

    rows = lax.broadcasted_iota(jnp.int32, (16, 128), 0)

    def block(m, b):
        return (pltpu.roll(m, 128 - 16 * b, 1) if b else m)[:, :16]

    trial = unpack(summed(trial3, trial_copies))
    m = jnp.where(lane < 32, trial, jnp.where(lane == rows + 32, 1.0, 0.0))
    for i in range(16):
        pivot_row = m[i:i + 1, :] / m[i:i + 1, i:i + 1]
        m = jnp.where(rows == i, pivot_row, m - m[:, i:i + 1] * pivot_row)
    inv_b, inv_b_ttd = block(m, 2), block(m, 1)
    ttd, tdtd = block(trial, 1), block(trial, 2)

    red2[z] = summed(red1, copies)
    total = unpack(summed(red2, to_planes(red2, r2_s, r2_r)))
    total_ref[...] = total
    inverse_ref[...] = m
    trial_ref[...] = trial
    states_ref[...] = jnp.concatenate([both, ad], axis=0)

    for c in [*far.values(), *passed, *sent, *along_x.values(), *across.values(), *sums]:
        c.wait_send()


def finish(total_ref, inverse_ref, trial_ref, states_ref, new_ref, ritz_ref):
    lane = lax.broadcasted_iota(jnp.int32, (16, 128), 1)
    rows = lax.broadcasted_iota(jnp.int32, (16, 128), 0)

    def block(m, b):
        return (pltpu.roll(m, 128 - 16 * b, 1) if b else m)[:, :16]

    total = total_ref[...]
    inv_b, inv_b_ttd = block(inverse_ref[...], 2), block(inverse_ref[...], 1)
    ttd, tdtd = block(trial_ref[...], 1), block(trial_ref[...], 2)
    both, ad = states_ref[:32], states_ref[32:]
    dot = functools.partial(jnp.dot, precision=HI, preferred_element_type=F32)
    solved = dot(inv_b, total)
    coef = block(solved, 0)
    tda = block(total, 2)
    level = dot(jnp.concatenate([ttd, inv_b_ttd, tdtd], axis=0), coef)
    corr = block(total, 1) - level[:16]
    mixing = block(solved, 1) - level[16:32]
    inner = level[32:48] - tda
    tn = (((0,), (0,)), ((), ()))
    gram = block(total, 3) + lax.dot_general(jnp.concatenate([-tda, coef, -corr], axis=0),
                                             jnp.concatenate([coef, inner, mixing], axis=0), tn,
                                             precision=HI, preferred_element_type=F32)
    gram = gram / TOTAL_ROWS
    projected = ad - lax.dot_general(jnp.concatenate([mixing, coef], axis=0), both, tn,
                                     precision=HI, preferred_element_type=F32)
    small = (16, 16)
    diagonal = lax.broadcasted_iota(jnp.int32, small, 0) == lax.broadcasted_iota(jnp.int32, small, 1)
    ritz_ref[...] = jnp.sum(jnp.where(diagonal, coef, 0.0), axis=0)

    e = jnp.concatenate([gram, jnp.where(diagonal, 1.0, 0.0), jnp.zeros((16, 96), F32)], axis=1)
    for i in range(15):
        e = e - jnp.where(rows > i, e[:, i:i + 1] / e[i:i + 1, i:i + 1], 0.0) * e[i:i + 1, :]
    pivots = jnp.sum(jnp.where(rows == lane, e, 0.0), axis=1, keepdims=True)
    inv_factor = block(e * lax.rsqrt(pivots), 1)
    new = jnp.dot(inv_factor, projected, precision=HI, preferred_element_type=F32)
    for p in range(16):
        half = new[:, (p // 8) * 128:(p // 8 + 1) * 128]
        g = p % 8
        new_ref[p] = (pltpu.roll(half, 128 - 16 * g, 1) if g else half)[:, :16]


def body(trial_block, ham_blocks, partners, stored_at, precond_diag):
    vmem = pl.BlockSpec(memory_space=pltpu.VMEM)
    hbm = pl.BlockSpec(memory_space=pltpu.HBM)
    dma = pltpu.SemaphoreType.DMA
    n_chunks = NJ // CHUNK
    counts = (5, 16, 16, 18, 18, 3 * n_chunks, 3 * n_chunks, 4 * n_chunks, 4 * n_chunks, 7, 7, 3, 3, 16, 16, 31, 31, 16, 16)
    vm4 = [vmem] * 4
    parts = pl.pallas_call(
        kernel,
        out_shape=[jax.ShapeDtypeStruct(shape, F32) for shape in ((16, 128), (16, 128), (16, 128), (48, 256))],
        in_specs=[hbm] * 5,
        out_specs=vm4,
        scratch_shapes=[
            pltpu.VMEM((16, 16, 16), F32),
            pltpu.VMEM((16, 16), F32),
            pltpu.VMEM((16, 8, 16, 128), BF16),
            pltpu.SMEM((8, 16), jnp.int32),
            pltpu.SMEM((1024,), jnp.int32),
            pltpu.SMEM((256,), jnp.int32),
            pltpu.VMEM((64, 2, 16, 128), BF16),
            pltpu.VMEM((8, 8, 16, 256), BF16),
            *[pltpu.VMEM((n, 8, 128), F32) for n in (8, 4, 16, 32, 16)],
            *[dma((n,)) for n in counts],
        ],
        compiler_params=pltpu.CompilerParams(collective_id=0, has_side_effects=True, vmem_limit_bytes=60 * 2**20),
    )(trial_block, ham_blocks, partners.T, stored_at, precond_diag)
    new_block, ritz = pl.pallas_call(
        finish,
        out_shape=(jax.ShapeDtypeStruct((16, 16, 16), F32), jax.ShapeDtypeStruct((16,), F32)),
        in_specs=vm4,
        out_specs=(vmem, vmem),
        compiler_params=pltpu.CompilerParams(vmem_limit_bytes=60 * 2**20),
    )(*parts)
    return new_block, ritz


def solution(mesh):
    return jax.shard_map(
        body,
        mesh=mesh,
        in_specs=(
            P("chan", None, "rad"),
            P("chan", None, "rad", None),
            P("chan", None),
            P(),
            P("chan", "rad"),
        ),
        out_specs=(P("chan", None, "rad"), P()),
        check_vma=False,
    )
```

```python
import functools

import jax
import jax.numpy as jnp
from jax import lax
from jax.experimental import pallas as pl
from jax.experimental.pallas import tpu as pltpu
from jax.sharding import PartitionSpec as P

MESH = pl.DeviceIdType.MESH
HI = lax.Precision.HIGHEST
F32 = jnp.float32
BF16 = jnp.bfloat16
TOTAL_ROWS = 1024.0 * 128.0
NJ = 8
NEAR_Z = (4, 12, 3, 13, 2, 14, 1, 15)
ALONG_Z = (8, 7, 9, 6, 10, 5, 11, 4, 12, 3, 13, 2, 14, 1, 15)
IN_PLANE = sorted(((dy, dr) for dy in range(4) for dr in range(8) if dy or dr),
                  key=lambda d: -((0, 1, 2, 1)[d[0]] + (0, 1, 2, 1)[d[1] // 2]))
CHUNK = 4


def kernel(t_hbm, ham_hbm, partners_hbm, stored_hbm, d_hbm, total_ref, inverse_ref, trial_ref, states_ref,
           t_ref, d_ref, hbuf, partners_ref, stored_ref, place, tbl, yall, trial1, trial2, trial3, red1, red2,
           in_sem, far_s, far_r, own_s, own_r, x_s, x_r, c_s, c_r,
           t1_s, t1_r, t2_s, t2_r, t3_s, t3_r, r1_s, r1_r, r2_s, r2_r):
    chan = lax.axis_index("chan")
    rad = lax.axis_index("rad")
    z, y = chan // 4, chan % 4

    def at(dz, yy):
        return (((z + dz + 16) % 16) * 4 + yy, rad)

    t_copy = pltpu.make_async_copy(t_hbm, t_ref, in_sem.at[0])
    t_copy.start()
    barrier = pltpu.get_barrier_semaphore()
    for m in NEAR_Z:
        pl.semaphore_signal(barrier, inc=1, device_id=at(m, y), device_id_type=MESH)
    for k in (2, 1, 3):
        pl.semaphore_signal(barrier, inc=1, device_id=at(0, y ^ k), device_id_type=MESH)
    for i in range(1, 8):
        pl.semaphore_signal(barrier, inc=1, device_id=(chan, rad ^ i), device_id_type=MESH)
    rest = [pltpu.make_async_copy(src, dst, in_sem.at[i + 1]) for i, (src, dst) in enumerate(
        ((d_hbm, d_ref), (partners_hbm, partners_ref), (stored_hbm, stored_ref), (ham_hbm, hbuf)))]
    for c in rest:
        c.start()

    t_copy.wait()
    t2d = t_ref[...].reshape(256, 16)
    eye = (lax.broadcasted_iota(jnp.int32, (16, 16), 0) == lax.broadcasted_iota(jnp.int32, (16, 16), 1)).astype(BF16)
    turned = lax.dot_general(eye, t2d.astype(BF16), (((1,), (1,)), ((), ())), preferred_element_type=F32).astype(BF16)
    tbl[y * 16, 0] = turned[:, :128]
    tbl[y * 16, 1] = turned[:, 128:]

    pl.semaphore_wait(barrier, len(NEAR_Z) + 3 + 7)

    def remote(src, dst, s, r, dev):
        copy = pltpu.make_async_remote_copy(src_ref=src, dst_ref=dst, send_sem=s, recv_sem=r,
                                            device_id=dev, device_id_type=MESH)
        copy.start()
        return copy

    def blocks(first, end):
        return tbl.at[pl.ds(y * 16 + first, end - first)]

    far = {}
    for m in NEAR_Z:
        far[16 - m] = remote(blocks(0, 1), blocks(16 - m, 17 - m), far_s.at[m], far_r.at[m], at(m, y))

    for c in rest:
        c.wait()
    t2 = jnp.concatenate([t_ref[p] for p in range(16)], axis=1)
    d2 = jnp.concatenate([d_ref[p:p + 1, :] for p in range(16)], axis=1)
    td = t2 / d2

    def pack(m):
        left_half = lax.broadcasted_iota(jnp.int32, (8, 128), 1) < 64
        return jnp.where(left_half, m[:8], pltpu.roll(m[8:], 64, 1))

    def unpack(m):
        return jnp.concatenate([m, pltpu.roll(m, 64, 1)], axis=0)

    def widen(m):
        return jnp.concatenate([m, jnp.zeros((m.shape[0], 128 - m.shape[1]), F32)], axis=1)

    sums = []

    def to_plane(buf, s, r):
        piece = buf.at[pl.ds(y * 8 + rad, 1)]
        return [remote(piece, piece, s.at[i], r.at[i], (z * 4 + (y ^ dy), rad ^ dr))
                for i, (dy, dr) in enumerate(IN_PLANE)]

    def to_rad(buf, s, r):
        piece = buf.at[pl.ds(rad, 1)]
        return [remote(piece, piece, s.at[i - 1], r.at[i - 1], (chan, rad ^ i)) for i in range(1, 8)]

    def to_y(buf, s, r):
        piece = buf.at[pl.ds(y, 1)]
        return [remote(piece, piece, s.at[k - 1], r.at[k - 1], at(0, y ^ k)) for k in (2, 1, 3)]

    def to_planes(buf, s, r):
        piece = buf.at[pl.ds(z, 1)]
        return [remote(piece, piece, s.at[m], r.at[m], at(m, y)) for m in ALONG_Z]

    def summed(buf, copies):
        for c in copies:
            c.wait_recv()
        sums.extend(copies)
        parts = [buf[i] for i in range(buf.shape[0])]
        while len(parts) > 1:
            parts = [u + v for u, v in zip(parts[::2], parts[1::2])]
        return parts[0]

    lane = lax.broadcasted_iota(jnp.int32, (16, 128), 1)
    nt = (((1,), (1,)), ((), ()))

    both = jnp.concatenate([t2, td], axis=0)
    prods = widen(lax.dot_general(both, both, nt, precision=HI, preferred_element_type=F32))
    prods = jnp.where(lane < 32, prods[:16], jnp.where(lane < 48, pltpu.roll(prods[16:], 16, 1), 0.0))
    trial1[rad] = pack(prods)
    trial_copies = to_rad(trial1, t1_s, t1_r)

    def locate(j, carry):
        for p in range(16):
            row = stored_ref[partners_ref[j, p]]
            ahead = (row // 64 - z + 16) % 16
            place[j * 16 + p] = ((row // 16) % 4 * 16 + ahead) * 2 + (row // 8) % 2
            place[128 + j * 16 + p] = ((p - row + 16) % 8) * 16
        return carry

    lax.fori_loop(0, NJ, locate, 0)

    sent, passed = [], []

    def along_y(first, end, g):
        for k in (2, 1, 3):
            i = g * 3 + k - 1
            sent.append(remote(blocks(first, end), blocks(first, end), own_s.at[i], own_r.at[i], at(0, y ^ k)))

    for n, (take, first, end, to, dz) in enumerate((
            ((15, 14), 14, 16, 10, 4), ((1, 2), 1, 3, 5, -4), ((13,), 13, 14, 9, 4), ((3, 4), 3, 5, 7, -4))):
        for i in take:
            far[i].wait_recv()
        passed.append(remote(blocks(first, end), blocks(to, to + end - first), far_s.at[5 + n], far_r.at[5 + n], at(dz, y)))
    along_y(0, 5, 0)
    far[12].wait_recv()
    along_y(12, 16, 1)
    trial2[y] = summed(trial1, trial_copies)
    trial_copies = to_y(trial2, t2_s, t2_r)
    for n, (first, end) in enumerate(((10, 12), (5, 7), (9, 10), (7, 9))):
        passed[n].wait_recv()
        along_y(first, end, 2 + n)
    for c in sent:
        c.wait_recv()

    lane_group = lax.broadcasted_iota(jnp.int32, (16, 128), 1) // 16

    def select(j, carry):
        for hp in range(2):
            acc = jnp.zeros((16, 128), F32)
            for g in range(8):
                i = j * 16 + hp * 8 + g
                moved = pltpu.roll(tbl[place[i] // 2, place[i] % 2].astype(F32), place[128 + i], 1)
                acc = jnp.where(lane_group == g, moved, acc)
            yall[j, rad, :, hp * 128:(hp + 1) * 128] = acc.astype(BF16)
        return carry

    other = (chan, rad ^ 1)
    along_x, across = {}, {}
    n_chunks = NJ // CHUNK
    for c in range(n_chunks):
        lax.fori_loop(c * CHUNK, (c + 1) * CHUNK, select, 0)
        piece = yall.at[pl.ds(c * CHUNK, CHUNK), pl.ds(rad, 1)]
        for i in (2, 1, 3):
            k = c * 3 + i - 1
            along_x[c, i] = remote(piece, piece, x_s.at[k], x_r.at[k], (chan, rad ^ (2 * i)))
        across[c, 0] = remote(piece, piece, c_s.at[c * 4], c_r.at[c * 4], other)

    trial3[z] = summed(trial2, trial_copies)
    trial_copies = to_planes(trial3, t3_s, t3_r)
    out_group = lax.broadcasted_iota(jnp.int32, (16, 256), 1) // 16
    applied_r = jnp.zeros((16, 256), F32)
    for c in range(n_chunks + 1):
        if c < n_chunks:
            for i in (1, 3, 2):
                along_x[c, i].wait_recv()
                piece = yall.at[pl.ds(c * CHUNK, CHUNK), pl.ds(rad ^ (2 * i), 1)]
                across[c, i] = remote(piece, piece, c_s.at[c * 4 + i], c_r.at[c * 4 + i], other)
        if c:
            for i in range(4):
                across[c - 1, i].wait_recv()
            js = range((c - 1) * CHUNK, c * CHUNK)
            left = jnp.concatenate([hbuf[:, j].reshape(256, 128) for j in js], axis=1)
            right = yall[(c - 1) * CHUNK:c * CHUNK].reshape(CHUNK * 128, 256)
            out = jnp.dot(left, right, preferred_element_type=F32)
            for p in range(16):
                applied_r += jnp.where(out_group == p, out[p * 16:(p + 1) * 16, :], 0.0)

    turned_a = applied_r.T
    a2 = jnp.concatenate([turned_a[p * 16:(p + 1) * 16, :] for p in range(16)], axis=1)
    ad = a2 / d2

    prods = widen(lax.dot_general(jnp.concatenate([both, ad], axis=0), jnp.concatenate([a2, ad], axis=0), nt,
                                  precision=HI, preferred_element_type=F32))
    prods = jnp.where(lane < 32, prods[:16],
                      jnp.where(lane < 48, pltpu.roll(prods[16:32], 16, 1), pltpu.roll(prods[32:], 32, 1)))
    red1[y * 8 + rad] = pack(prods)
    copies = to_plane(red1, r1_s, r1_r)

    rows = lax.broadcasted_iota(jnp.int32, (16, 128), 0)

    def block(m, b):
        return (pltpu.roll(m, 128 - 16 * b, 1) if b else m)[:, :16]

    trial = unpack(summed(trial3, trial_copies))
    m = jnp.where(lane < 32, trial, jnp.where(lane == rows + 32, 1.0, 0.0))
    for i in range(16):
        pivot_row = m[i:i + 1, :] / m[i:i + 1, i:i + 1]
        m = jnp.where(rows == i, pivot_row, m - m[:, i:i + 1] * pivot_row)
    inv_b, inv_b_ttd = block(m, 2), block(m, 1)
    ttd, tdtd = block(trial, 1), block(trial, 2)

    red2[z] = summed(red1, copies)
    copies = to_planes(red2, r2_s, r2_r)
    for c in [*far.values(), *passed, *sent, *along_x.values(), *across.values(), *sums]:
        c.wait_send()
    total = unpack(summed(red2, copies))
    total_ref[...] = total
    inverse_ref[...] = m
    trial_ref[...] = trial
    states_ref[...] = jnp.concatenate([both, ad], axis=0)

    for c in copies:
        c.wait_send()


def finish(total_ref, inverse_ref, trial_ref, states_ref, new_ref, ritz_ref):
    lane = lax.broadcasted_iota(jnp.int32, (16, 128), 1)
    rows = lax.broadcasted_iota(jnp.int32, (16, 128), 0)

    def block(m, b):
        return (pltpu.roll(m, 128 - 16 * b, 1) if b else m)[:, :16]

    total = total_ref[...]
    inv_b, inv_b_ttd = block(inverse_ref[...], 2), block(inverse_ref[...], 1)
    ttd, tdtd = block(trial_ref[...], 1), block(trial_ref[...], 2)
    both, ad = states_ref[:32], states_ref[32:]
    dot = functools.partial(jnp.dot, precision=HI, preferred_element_type=F32)
    solved = dot(inv_b, total)
    coef = block(solved, 0)
    tda = block(total, 2)
    level = dot(jnp.concatenate([ttd, inv_b_ttd, tdtd], axis=0), coef)
    corr = block(total, 1) - level[:16]
    mixing = block(solved, 1) - level[16:32]
    inner = level[32:48] - tda
    tn = (((0,), (0,)), ((), ()))
    gram = block(total, 3) + lax.dot_general(jnp.concatenate([-tda, coef, -corr], axis=0),
                                             jnp.concatenate([coef, inner, mixing], axis=0), tn,
                                             precision=HI, preferred_element_type=F32)
    gram = gram / TOTAL_ROWS
    projected = ad - lax.dot_general(jnp.concatenate([mixing, coef], axis=0), both, tn,
                                     precision=HI, preferred_element_type=F32)
    small = (16, 16)
    diagonal = lax.broadcasted_iota(jnp.int32, small, 0) == lax.broadcasted_iota(jnp.int32, small, 1)
    ritz_ref[...] = jnp.sum(jnp.where(diagonal, coef, 0.0), axis=0)

    e = jnp.concatenate([gram, jnp.where(diagonal, 1.0, 0.0), jnp.zeros((16, 96), F32)], axis=1)
    for i in range(15):
        e = e - jnp.where(rows > i, e[:, i:i + 1], 0.0) * (e[i:i + 1, :] / e[i:i + 1, i:i + 1])
    pivots = jnp.sum(jnp.where(rows == lane, e, 0.0), axis=1, keepdims=True)
    inv_factor = block(e * lax.rsqrt(pivots), 1)
    new = jnp.dot(inv_factor, projected, precision=HI, preferred_element_type=F32)
    for p in range(16):
        half = new[:, (p // 8) * 128:(p // 8 + 1) * 128]
        g = p % 8
        new_ref[p] = (pltpu.roll(half, 128 - 16 * g, 1) if g else half)[:, :16]


def body(trial_block, ham_blocks, partners, stored_at, precond_diag):
    vmem = pl.BlockSpec(memory_space=pltpu.VMEM)
    hbm = pl.BlockSpec(memory_space=pltpu.HBM)
    dma = pltpu.SemaphoreType.DMA
    n_chunks = NJ // CHUNK
    counts = (5, 16, 16, 18, 18, 3 * n_chunks, 3 * n_chunks, 4 * n_chunks, 4 * n_chunks, 7, 7, 3, 3, 16, 16, 31, 31, 16, 16)
    vm4 = [vmem] * 4
    parts = pl.pallas_call(
        kernel,
        out_shape=[jax.ShapeDtypeStruct(shape, F32) for shape in ((16, 128), (16, 128), (16, 128), (48, 256))],
        in_specs=[hbm] * 5,
        out_specs=vm4,
        scratch_shapes=[
            pltpu.VMEM((16, 16, 16), F32),
            pltpu.VMEM((16, 16), F32),
            pltpu.VMEM((16, 8, 16, 128), BF16),
            pltpu.SMEM((8, 16), jnp.int32),
            pltpu.SMEM((1024,), jnp.int32),
            pltpu.SMEM((256,), jnp.int32),
            pltpu.VMEM((64, 2, 16, 128), BF16),
            pltpu.VMEM((8, 8, 16, 256), BF16),
            *[pltpu.VMEM((n, 8, 128), F32) for n in (8, 4, 16, 32, 16)],
            *[dma((n,)) for n in counts],
        ],
        compiler_params=pltpu.CompilerParams(collective_id=0, has_side_effects=True, vmem_limit_bytes=60 * 2**20),
    )(trial_block, ham_blocks, partners.T, stored_at, precond_diag)
    new_block, ritz = pl.pallas_call(
        finish,
        out_shape=(jax.ShapeDtypeStruct((16, 16, 16), F32), jax.ShapeDtypeStruct((16,), F32)),
        in_specs=vm4,
        out_specs=(vmem, vmem),
        compiler_params=pltpu.CompilerParams(vmem_limit_bytes=60 * 2**20),
    )(*parts)
    return new_block, ritz


def solution(mesh):
    return jax.shard_map(
        body,
        mesh=mesh,
        in_specs=(
            P("chan", None, "rad"),
            P("chan", None, "rad", None),
            P("chan", None),
            P(),
            P("chan", "rad"),
        ),
        out_specs=(P("chan", None, "rad"), P()),
        check_vma=False,
    )
```

```python
import functools

import jax
import jax.numpy as jnp
from jax import lax
from jax.experimental import pallas as pl
from jax.experimental.pallas import tpu as pltpu
from jax.sharding import PartitionSpec as P

MESH = pl.DeviceIdType.MESH
HI = lax.Precision.HIGHEST
F32 = jnp.float32
BF16 = jnp.bfloat16
TOTAL_ROWS = 1024.0 * 128.0
NJ = 8
NEAR_Z = (4, 12, 3, 13, 2, 14, 1, 15)
ALONG_Z = (8, 7, 9, 6, 10, 5, 11, 4, 12, 3, 13, 2, 14, 1, 15)
IN_PLANE = sorted(((dy, dr) for dy in range(4) for dr in range(8) if dy or dr),
                  key=lambda d: -((0, 1, 2, 1)[d[0]] + (0, 1, 2, 1)[d[1] // 2]))
CHUNK = 4


def kernel(t_hbm, ham_hbm, partners_hbm, stored_hbm, d_hbm, total_ref, inverse_ref, trial_ref, states_ref,
           t_ref, d_ref, hbuf, partners_ref, stored_ref, place, tbl, yall, trial1, trial2, trial3, red1, red2,
           in_sem, far_s, far_r, own_s, own_r, x_s, x_r, c_s, c_r,
           t1_s, t1_r, t2_s, t2_r, t3_s, t3_r, r1_s, r1_r, r2_s, r2_r):
    chan = lax.axis_index("chan")
    rad = lax.axis_index("rad")
    z, y = chan // 4, chan % 4

    def at(dz, yy):
        return (((z + dz + 16) % 16) * 4 + yy, rad)

    t_copy = pltpu.make_async_copy(t_hbm, t_ref, in_sem.at[0])
    t_copy.start()
    barrier = pltpu.get_barrier_semaphore()
    for m in NEAR_Z:
        pl.semaphore_signal(barrier, inc=1, device_id=at(m, y), device_id_type=MESH)
    for k in (2, 1, 3):
        pl.semaphore_signal(barrier, inc=1, device_id=at(0, y ^ k), device_id_type=MESH)
    for i in range(1, 8):
        pl.semaphore_signal(barrier, inc=1, device_id=(chan, rad ^ i), device_id_type=MESH)
    rest = [pltpu.make_async_copy(src, dst, in_sem.at[i + 1]) for i, (src, dst) in enumerate(
        ((d_hbm, d_ref), (partners_hbm, partners_ref), (stored_hbm, stored_ref), (ham_hbm, hbuf)))]
    for c in rest:
        c.start()

    t_copy.wait()
    t2d = t_ref[...].reshape(256, 16)
    eye = (lax.broadcasted_iota(jnp.int32, (16, 16), 0) == lax.broadcasted_iota(jnp.int32, (16, 16), 1)).astype(BF16)
    turned = lax.dot_general(eye, t2d.astype(BF16), (((1,), (1,)), ((), ())), preferred_element_type=F32).astype(BF16)
    tbl[y * 16, 0] = turned[:, :128]
    tbl[y * 16, 1] = turned[:, 128:]

    pl.semaphore_wait(barrier, len(NEAR_Z) + 3 + 7)

    def remote(src, dst, s, r, dev):
        copy = pltpu.make_async_remote_copy(src_ref=src, dst_ref=dst, send_sem=s, recv_sem=r,
                                            device_id=dev, device_id_type=MESH)
        copy.start()
        return copy

    def blocks(first, end):
        return tbl.at[pl.ds(y * 16 + first, end - first)]

    far = {}
    for m in NEAR_Z:
        far[16 - m] = remote(blocks(0, 1), blocks(16 - m, 17 - m), far_s.at[m], far_r.at[m], at(m, y))

    for c in rest:
        c.wait()
    t2 = jnp.concatenate([t_ref[p] for p in range(16)], axis=1)
    d2 = jnp.concatenate([d_ref[p:p + 1, :] for p in range(16)], axis=1)
    td = t2 / d2

    def pack(m):
        left_half = lax.broadcasted_iota(jnp.int32, (8, 128), 1) < 64
        return jnp.where(left_half, m[:8], pltpu.roll(m[8:], 64, 1))

    def unpack(m):
        return jnp.concatenate([m, pltpu.roll(m, 64, 1)], axis=0)

    def widen(m):
        return jnp.concatenate([m, jnp.zeros((m.shape[0], 128 - m.shape[1]), F32)], axis=1)

    sums = []

    def to_plane(buf, s, r):
        piece = buf.at[pl.ds(y * 8 + rad, 1)]
        return [remote(piece, piece, s.at[i], r.at[i], (z * 4 + (y ^ dy), rad ^ dr))
                for i, (dy, dr) in enumerate(IN_PLANE)]

    def to_rad(buf, s, r):
        piece = buf.at[pl.ds(rad, 1)]
        return [remote(piece, piece, s.at[i - 1], r.at[i - 1], (chan, rad ^ i)) for i in range(1, 8)]

    def to_y(buf, s, r):
        piece = buf.at[pl.ds(y, 1)]
        return [remote(piece, piece, s.at[k - 1], r.at[k - 1], at(0, y ^ k)) for k in (2, 1, 3)]

    def to_planes(buf, s, r):
        piece = buf.at[pl.ds(z, 1)]
        return [remote(piece, piece, s.at[m], r.at[m], at(m, y)) for m in ALONG_Z]

    def summed(buf, copies):
        for c in copies:
            c.wait_recv()
        sums.extend(copies)
        parts = [buf[i] for i in range(buf.shape[0])]
        while len(parts) > 1:
            parts = [u + v for u, v in zip(parts[::2], parts[1::2])]
        return parts[0]

    lane = lax.broadcasted_iota(jnp.int32, (16, 128), 1)
    nt = (((1,), (1,)), ((), ()))

    both = jnp.concatenate([t2, td], axis=0)
    prods = widen(lax.dot_general(both, both, nt, precision=HI, preferred_element_type=F32))
    prods = jnp.where(lane < 32, prods[:16], jnp.where(lane < 48, pltpu.roll(prods[16:], 16, 1), 0.0))
    trial1[rad] = pack(prods)
    trial_copies = to_rad(trial1, t1_s, t1_r)

    def locate(j, carry):
        for p in range(16):
            row = stored_ref[partners_ref[j, p]]
            ahead = (row // 64 - z + 16) % 16
            place[j * 16 + p] = ((row // 16) % 4 * 16 + ahead) * 2 + (row // 8) % 2
            place[128 + j * 16 + p] = ((p - row + 16) % 8) * 16
        return carry

    lax.fori_loop(0, NJ, locate, 0)

    sent, passed = [], []

    def along_y(first, end, g):
        for k in (2, 1, 3):
            i = g * 3 + k - 1
            sent.append(remote(blocks(first, end), blocks(first, end), own_s.at[i], own_r.at[i], at(0, y ^ k)))

    for n, (take, first, end, to, dz) in enumerate((
            ((15, 14), 14, 16, 10, 4), ((1, 2), 1, 3, 5, -4), ((13,), 13, 14, 9, 4), ((3, 4), 3, 5, 7, -4))):
        for i in take:
            far[i].wait_recv()
        passed.append(remote(blocks(first, end), blocks(to, to + end - first), far_s.at[5 + n], far_r.at[5 + n], at(dz, y)))
    along_y(0, 5, 0)
    far[12].wait_recv()
    along_y(12, 16, 1)
    for n, (first, end) in enumerate(((10, 12), (5, 7), (9, 10), (7, 9))):
        passed[n].wait_recv()
        along_y(first, end, 2 + n)
    trial2[y] = summed(trial1, trial_copies)
    trial_copies = to_y(trial2, t2_s, t2_r)
    for c in sent:
        c.wait_recv()

    lane_group = lax.broadcasted_iota(jnp.int32, (16, 128), 1) // 16

    def select(j, carry):
        for hp in range(2):
            acc = jnp.zeros((16, 128), F32)
            for g in range(8):
                i = j * 16 + hp * 8 + g
                moved = pltpu.roll(tbl[place[i] // 2, place[i] % 2].astype(F32), place[128 + i], 1)
                acc = jnp.where(lane_group == g, moved, acc)
            yall[j, rad, :, hp * 128:(hp + 1) * 128] = acc.astype(BF16)
        return carry

    other = (chan, rad ^ 1)
    along_x, across = {}, {}
    n_chunks = NJ // CHUNK
    for c in range(n_chunks):
        lax.fori_loop(c * CHUNK, (c + 1) * CHUNK, select, 0)
        piece = yall.at[pl.ds(c * CHUNK, CHUNK), pl.ds(rad, 1)]
        for i in (2, 1, 3):
            k = c * 3 + i - 1
            along_x[c, i] = remote(piece, piece, x_s.at[k], x_r.at[k], (chan, rad ^ (2 * i)))
        across[c, 0] = remote(piece, piece, c_s.at[c * 4], c_r.at[c * 4], other)

    trial3[z] = summed(trial2, trial_copies)
    trial_copies = to_planes(trial3, t3_s, t3_r)
    out_group = lax.broadcasted_iota(jnp.int32, (16, 256), 1) // 16
    applied_r = jnp.zeros((16, 256), F32)
    for c in range(n_chunks + 1):
        if c < n_chunks:
            for i in (1, 3, 2):
                along_x[c, i].wait_recv()
                piece = yall.at[pl.ds(c * CHUNK, CHUNK), pl.ds(rad ^ (2 * i), 1)]
                across[c, i] = remote(piece, piece, c_s.at[c * 4 + i], c_r.at[c * 4 + i], other)
        if c:
            for i in range(4):
                across[c - 1, i].wait_recv()
            js = range((c - 1) * CHUNK, c * CHUNK)
            left = jnp.concatenate([hbuf[:, j].reshape(256, 128) for j in js], axis=1)
            right = yall[(c - 1) * CHUNK:c * CHUNK].reshape(CHUNK * 128, 256)
            out = jnp.dot(left, right, preferred_element_type=F32)
            for p in range(16):
                applied_r += jnp.where(out_group == p, out[p * 16:(p + 1) * 16, :], 0.0)

    turned_a = applied_r.T
    a2 = jnp.concatenate([turned_a[p * 16:(p + 1) * 16, :] for p in range(16)], axis=1)
    ad = a2 / d2

    prods = widen(lax.dot_general(jnp.concatenate([both, ad], axis=0), jnp.concatenate([a2, ad], axis=0), nt,
                                  precision=HI, preferred_element_type=F32))
    prods = jnp.where(lane < 32, prods[:16],
                      jnp.where(lane < 48, pltpu.roll(prods[16:32], 16, 1), pltpu.roll(prods[32:], 32, 1)))
    red1[y * 8 + rad] = pack(prods)
    copies = to_plane(red1, r1_s, r1_r)

    rows = lax.broadcasted_iota(jnp.int32, (16, 128), 0)

    def block(m, b):
        return (pltpu.roll(m, 128 - 16 * b, 1) if b else m)[:, :16]

    trial = unpack(summed(trial3, trial_copies))
    m = jnp.where(lane < 32, trial, jnp.where(lane == rows + 32, 1.0, 0.0))
    for i in range(16):
        pivot_row = m[i:i + 1, :] / m[i:i + 1, i:i + 1]
        m = jnp.where(rows == i, pivot_row, m - m[:, i:i + 1] * pivot_row)
    inv_b, inv_b_ttd = block(m, 2), block(m, 1)
    ttd, tdtd = block(trial, 1), block(trial, 2)

    red2[z] = summed(red1, copies)
    copies = to_planes(red2, r2_s, r2_r)
    for c in [*far.values(), *passed, *sent, *along_x.values(), *across.values(), *sums]:
        c.wait_send()
    total = unpack(summed(red2, copies))
    total_ref[...] = total
    inverse_ref[...] = m
    trial_ref[...] = trial
    states_ref[...] = jnp.concatenate([both, ad], axis=0)

    for c in copies:
        c.wait_send()


def finish(total_ref, inverse_ref, trial_ref, states_ref, new_ref, ritz_ref):
    lane = lax.broadcasted_iota(jnp.int32, (16, 128), 1)
    rows = lax.broadcasted_iota(jnp.int32, (16, 128), 0)

    def block(m, b):
        return (pltpu.roll(m, 128 - 16 * b, 1) if b else m)[:, :16]

    total = total_ref[...]
    inv_b, inv_b_ttd = block(inverse_ref[...], 2), block(inverse_ref[...], 1)
    ttd, tdtd = block(trial_ref[...], 1), block(trial_ref[...], 2)
    both, ad = states_ref[:32], states_ref[32:]
    dot = functools.partial(jnp.dot, precision=HI, preferred_element_type=F32)
    solved = dot(inv_b, total)
    coef = block(solved, 0)
    tda = block(total, 2)
    level = dot(jnp.concatenate([ttd, inv_b_ttd, tdtd], axis=0), coef)
    corr = block(total, 1) - level[:16]
    mixing = block(solved, 1) - level[16:32]
    inner = level[32:48] - tda
    tn = (((0,), (0,)), ((), ()))
    gram = block(total, 3) + lax.dot_general(jnp.concatenate([-tda, coef, -corr], axis=0),
                                             jnp.concatenate([coef, inner, mixing], axis=0), tn,
                                             precision=HI, preferred_element_type=F32)
    gram = gram / TOTAL_ROWS
    projected = ad - lax.dot_general(jnp.concatenate([mixing, coef], axis=0), both, tn,
                                     precision=HI, preferred_element_type=F32)
    small = (16, 16)
    diagonal = lax.broadcasted_iota(jnp.int32, small, 0) == lax.broadcasted_iota(jnp.int32, small, 1)
    ritz_ref[...] = jnp.sum(jnp.where(diagonal, coef, 0.0), axis=0)

    e = jnp.concatenate([gram, jnp.where(diagonal, 1.0, 0.0), jnp.zeros((16, 96), F32)], axis=1)
    for i in range(15):
        e = e - jnp.where(rows > i, e[:, i:i + 1], 0.0) * (e[i:i + 1, :] / e[i:i + 1, i:i + 1])
    pivots = jnp.sum(jnp.where(rows == lane, e, 0.0), axis=1, keepdims=True)
    inv_factor = block(e * lax.rsqrt(pivots), 1)
    new = jnp.dot(inv_factor, projected, precision=HI, preferred_element_type=F32)
    for p in range(16):
        half = new[:, (p // 8) * 128:(p // 8 + 1) * 128]
        g = p % 8
        new_ref[p] = (pltpu.roll(half, 128 - 16 * g, 1) if g else half)[:, :16]


def body(trial_block, ham_blocks, partners, stored_at, precond_diag):
    vmem = pl.BlockSpec(memory_space=pltpu.VMEM)
    hbm = pl.BlockSpec(memory_space=pltpu.HBM)
    dma = pltpu.SemaphoreType.DMA
    n_chunks = NJ // CHUNK
    counts = (5, 16, 16, 18, 18, 3 * n_chunks, 3 * n_chunks, 4 * n_chunks, 4 * n_chunks, 7, 7, 3, 3, 16, 16, 31, 31, 16, 16)
    vm4 = [vmem] * 4
    parts = pl.pallas_call(
        kernel,
        out_shape=[jax.ShapeDtypeStruct(shape, F32) for shape in ((16, 128), (16, 128), (16, 128), (48, 256))],
        in_specs=[hbm] * 5,
        out_specs=vm4,
        scratch_shapes=[
            pltpu.VMEM((16, 16, 16), F32),
            pltpu.VMEM((16, 16), F32),
            pltpu.VMEM((16, 8, 16, 128), BF16),
            pltpu.SMEM((8, 16), jnp.int32),
            pltpu.SMEM((1024,), jnp.int32),
            pltpu.SMEM((256,), jnp.int32),
            pltpu.VMEM((64, 2, 16, 128), BF16),
            pltpu.VMEM((8, 8, 16, 256), BF16),
            *[pltpu.VMEM((n, 8, 128), F32) for n in (8, 4, 16, 32, 16)],
            *[dma((n,)) for n in counts],
        ],
        compiler_params=pltpu.CompilerParams(collective_id=0, has_side_effects=True, vmem_limit_bytes=60 * 2**20),
    )(trial_block, ham_blocks, partners.T, stored_at, precond_diag)
    new_block, ritz = pl.pallas_call(
        finish,
        out_shape=(jax.ShapeDtypeStruct((16, 16, 16), F32), jax.ShapeDtypeStruct((16,), F32)),
        in_specs=vm4,
        out_specs=(vmem, vmem),
        compiler_params=pltpu.CompilerParams(vmem_limit_bytes=60 * 2**20),
    )(*parts)
    return new_block, ritz


def solution(mesh):
    return jax.shard_map(
        body,
        mesh=mesh,
        in_specs=(
            P("chan", None, "rad"),
            P("chan", None, "rad", None),
            P("chan", None),
            P(),
            P("chan", "rad"),
        ),
        out_specs=(P("chan", None, "rad"), P()),
        check_vma=False,
    )
```
